256 devices in a mesh: row: 8 (over x, core), col: 32 (over z, y).
Axes of the slice: x: 4, y: 4, z: 8, core: 2. Of those that a mesh axis runs over, the one named last changes fastest.
Arguments:
- fields: bfloat16 [4, 64, 768, 1536], P(None, 'row', 'col'), may hold values from -1.5 to 3, as said below
- block_points: int32 [8, 32, 48, 256], P('row', 'col'), may hold values from 0 to 24575
- sample_weight: bfloat16 [8, 32, 48, 256], P('row', 'col'), may hold values from 0.099609375 to 1
- block_turbine: int32 [8, 32, 48], P('row'), may hold values from 0 to 399, as said below
- block_count: int32 [8, 32], P('row'), may hold values from 36 to 48, as said below
Outputs:
- tendency: bfloat16 [4, 64, 768, 1536], P(None, 'row', 'col')
- thrust: float32 [8, 32, 48, 256], P('row', 'col')
The draws below stay inside these ranges and needn't reach their ends.
Inputs may be any that keep to these rules, and one draw needn't show every extreme that they name: `block_turbine`: entry [r, c, :] lists the turbines of the blocks of the device at row index r and col index c; turbine t belongs to owner col index t mod 32. Of one device's 48 blocks at most 3 have turbines of one owner col index, and in every row index some owner col index gets exactly 3 blocks from every device of that row index. `block_count`: A device's live blocks are its first ones; some device has all of them live. `fields`: field 0 is the streamwise velocity.
All inputs are finite; a program needn't handle non-finite values.
Results may differ from the reference program's by a relative error of at most 0.0036.
Values may be sent and summed in bfloat16 or wider, within the bound.
A program may use at most 128 MiB of HBM per device.

```python
import math
import jax
import jax.numpy as jnp
from jax import lax

NX = 1536
NY = 768
LEV_DEV = 8
TURBINES = 400
BLOCKS_DEV = 48
SAMPLES = 256
NZ = 64
ROTOR_POINTS = 24576
N_ROW = 8
N_COL = 32


def shuffle_tail(device_key):
    return jax.random.permutation(device_key, N_COL - 1) + 1


def shuffle_blocks(device_key):
    return jax.random.permutation(device_key, BLOCKS_DEV)


def draw_fields(key, part):
    key = jax.random.fold_in(key, 1)
    first_key = jax.random.fold_in(key, 0)
    height = jnp.arange(NZ, dtype=jnp.float32) / max(NZ - 1, 1)
    profile = 0.5 * jnp.exp(jnp.log(3.0) * height)
    mean_flow = jnp.zeros((4, NZ, 1, 1), jnp.float32).at[0].set(profile[:, None, None])
    total = mean_flow + 0.5 * jnp.clip(jax.random.normal(first_key, (4, NZ, NY, NX)), -3.0, 3.0)
    return total.astype(jnp.bfloat16)


def draw_block_turbine(key, part):
    key = jax.random.fold_in(key, 2)
    first_key, second_key, third_key, fourth_key = jax.random.split(key, 4)
    devices_all = N_ROW * N_COL
    capacity = max(2, 2 * BLOCKS_DEV // N_COL)
    row_heads = jax.random.randint(first_key, (N_ROW, 1, 1), 0, N_COL)
    shuffled = jax.vmap(shuffle_tail)(jax.random.split(second_key, devices_all)).astype(jnp.int32)
    col_orders = jnp.concatenate([jnp.zeros((devices_all, 1), jnp.int32), shuffled], 1).reshape(N_ROW, N_COL, N_COL)
    slot_group = jnp.arange(BLOCKS_DEV, dtype=jnp.int32) // capacity
    target = (row_heads + col_orders[:, :, slot_group]) % N_COL
    mixing = jax.vmap(shuffle_blocks)(jax.random.split(third_key, devices_all)).reshape(N_ROW, N_COL, BLOCKS_DEV)
    target = jnp.take_along_axis(target, mixing.astype(jnp.int32), axis=2)
    picked = jax.random.randint(fourth_key, (N_ROW, N_COL, BLOCKS_DEV), 0, TURBINES // N_COL)
    return (target + N_COL * picked).astype(jnp.int32)


def draw_block_count(key, part):
    key = jax.random.fold_in(key, 3)
    first_key, second_key = jax.random.split(key)
    counts = jax.random.randint(first_key, (N_ROW * N_COL,), 3 * BLOCKS_DEV // 4, BLOCKS_DEV + 1)
    full_device = jax.random.randint(second_key, (), 0, N_ROW * N_COL)
    counts = counts.at[full_device].set(BLOCKS_DEV)
    return counts.reshape(N_ROW, N_COL).astype(jnp.int32)


def set_ends(values, key, smallest, top_value):
    spot = [jax.random.randint(jax.random.fold_in(key, axis), (), 0, length) for axis, length in enumerate(values.shape)]
    longest = values.shape.index(max(values.shape))
    next_to = spot[:longest] + [(spot[longest] + 1) % values.shape[longest]] + spot[longest + 1:]
    return values.at[tuple(spot)].set(smallest).at[tuple(next_to)].set(top_value)


def block_scale(rng, extent, pieces, low, top_value):
    factor_of, own = 1.0, jax.random.fold_in(rng, 6)
    for dim, parts in pieces:
        draws = jnp.exp(jax.random.uniform(jax.random.fold_in(own, dim), (parts,), jnp.float32, low / len(pieces), top_value / len(pieces)))
        factor_of = factor_of * jnp.repeat(draws, extent[dim] // parts).reshape([-1 if axis == dim else 1 for axis in range(len(extent))])
    return factor_of


def setup_inputs(seed: int = 0) -> dict:
    key_list = jax.random.split(jax.random.key(seed), 6)
    fields = draw_fields(jax.random.fold_in(key_list[5], 71), 0)
    block_points = set_ends(jax.random.randint(key_list[1], (N_ROW, N_COL, BLOCKS_DEV, SAMPLES), 0, ROTOR_POINTS), jax.random.fold_in(key_list[1], 1), 0, ROTOR_POINTS - 1).astype(jnp.int32)
    sample_weight = jnp.clip(jnp.exp(math.log(1.0) - 2.306499 * jax.random.uniform(key_list[2], (N_ROW, N_COL, BLOCKS_DEV, SAMPLES), jnp.float32) ** block_scale(key_list[2], (N_ROW, N_COL, BLOCKS_DEV, SAMPLES), ((0, 8), (1, 32)), -0.2, 0.2)), 0.099609375, 1.0).astype(jnp.bfloat16)
    block_turbine = draw_block_turbine(jax.random.fold_in(key_list[5], 71), 0)
    block_count = draw_block_count(jax.random.fold_in(key_list[5], 71), 0)
    return {"fields": fields, "block_points": block_points, "sample_weight": sample_weight, "block_turbine": block_turbine, "block_count": block_count}


CT_HALF = 2.0 / 3.0
BUOYANCY = 0.3
HIGHEST = lax.Precision.HIGHEST


def spectral_table(length):
    counter = jnp.arange(length, dtype=jnp.int32)
    offset = (counter[:, None] - counter[None, :]) % length
    phase_angle = offset.astype(jnp.float32) * (jnp.pi / length)
    parity = 1.0 - 2.0 * (offset % 2).astype(jnp.float32)
    sine_safe = jnp.where(offset == 0, 1.0, jnp.sin(phase_angle))
    entries = -(jnp.pi / length) * parity * jnp.cos(phase_angle) / sine_safe
    return jnp.where(offset == 0, 0.0, entries).astype(jnp.bfloat16)


def disk_thrust(fields, block_points, sample_weight, block_turbine, block_count):
    local_rows = NY // N_COL
    plane_size = local_rows * NX
    row_ids = jnp.arange(N_ROW, dtype=jnp.int32)[:, None, None, None]
    col_ids = jnp.arange(N_COL, dtype=jnp.int32)[None, :, None, None]
    level_of = row_ids * LEV_DEV + block_points // plane_size
    row_of = col_ids * local_rows + (block_points // NX) % local_rows
    column_of = block_points % NX
    sampled = fields[0][level_of, row_of, column_of].astype(jnp.float32)
    active = (jnp.arange(BLOCKS_DEV, dtype=jnp.int32)[None, None, :] < block_count[:, :, None]).astype(jnp.float32)
    weight = sample_weight.astype(jnp.float32) * active[..., None]
    moments = jnp.stack([jnp.sum(weight * sampled, -1), jnp.sum(weight, -1)], -1).reshape(-1, 2)
    onehot = (block_turbine.reshape(-1)[:, None] == jnp.arange(TURBINES, dtype=jnp.int32)[None, :]).astype(jnp.float32)
    totals = jnp.dot(onehot.T, moments, precision=HIGHEST)
    looked_up = jnp.dot(onehot, totals, precision=HIGHEST)
    inactive = 1.0 - active.reshape(-1)
    disk_speed = looked_up[:, 0] / (looked_up[:, 1] + inactive)
    thrust = -CT_HALF * (disk_speed * jnp.abs(disk_speed))[:, None] * weight.reshape(-1, SAMPLES)
    return level_of, row_of, column_of, thrust


def reference(fields, block_points, sample_weight, block_turbine, block_count):
    table_x = spectral_table(NX)
    table_y = spectral_table(NY)
    level_of, row_of, column_of, thrust = disk_thrust(fields, block_points, sample_weight, block_turbine, block_count)
    flat_plane = (row_of * NX + column_of).reshape(-1).astype(jnp.int32)
    flat_level = level_of.reshape(-1).astype(jnp.int32)
    flat_thrust = thrust.reshape(-1)

    def one_level(level_at):
        level_slab = lax.dynamic_index_in_dim(fields, level_at, 1, keepdims=False)
        slope_x = jnp.dot(level_slab.reshape(-1, NX), table_x, preferred_element_type=jnp.float32).reshape(4, NY, NX)
        turned = jnp.swapaxes(level_slab, 1, 2).reshape(-1, NY)
        slope_y = jnp.swapaxes(jnp.dot(turned, table_y, preferred_element_type=jnp.float32).reshape(4, NX, NY), 1, 2)
        across = level_slab[1].astype(jnp.float32)
        rounded = lax.optimization_barrier((across[None] * slope_y).astype(jnp.bfloat16))
        term_y = rounded.astype(jnp.float32)
        target = jnp.where(flat_level == level_at, flat_plane, NY * NX)
        forcing = jnp.zeros((NY * NX,), jnp.float32).at[target].add(flat_thrust, mode="drop").reshape(NY, NX)
        speed_field = level_slab[0].astype(jnp.float32)
        advect = -(speed_field[None] * slope_x) - term_y
        nothing = jnp.zeros((NY, NX), jnp.float32)
        source_terms = jnp.stack([forcing, nothing, BUOYANCY * level_slab[3].astype(jnp.float32), nothing])
        return (advect + source_terms).astype(jnp.bfloat16)

    stacked = lax.map(one_level, jnp.arange(NZ, dtype=jnp.int32))
    return jnp.swapaxes(stacked, 0, 1), thrust.reshape(N_ROW, N_COL, BLOCKS_DEV, SAMPLES)
```

```python
import functools

import jax
import jax.numpy as jnp
import ml_dtypes
import numpy as np
from jax import lax
from jax.experimental import pallas as pl
from jax.experimental.pallas import tpu as pltpu
from jax.sharding import PartitionSpec as P

MESH = pl.DeviceIdType.MESH
HBM = pl.BlockSpec(memory_space=pl.ANY)

N_ROW = 8
N_COL = 32
RING_Y = 4
RING_Z = 8
FIELDS = 4
NX = 1536
NY = 768
TURBINES = 400
BLOCKS = 48
SAMPLES = 256
LANES = 128
CT_HALF = 2.0 / 3.0
BUOYANCY = 0.3

ROWS = 768
PLANE = ROWS // FIELDS
PIECE = 2 * ROWS // N_COL
HALF = NX // 2
CHUNK = 256
CHUNKS = HALF // CHUNK
PENCIL = N_COL * PIECE
ROTOR_LINES = 16
ROTOR_TILES = NX // LANES
TURBINE_LANES = 512
BAND = 8 * PIECE


def spectral_row(length):
    offset = np.arange(length, dtype=np.int32)
    phase_angle = offset.astype(np.float32) * np.float32(np.pi / length)
    parity = np.float32(1.0) - np.float32(2.0) * (offset % 2).astype(np.float32)
    sine_safe = np.where(offset == 0, np.float32(1.0), np.sin(phase_angle))
    entries = np.float32(-(np.pi / length)) * parity * np.cos(phase_angle) / sine_safe
    entries = np.where(offset == 0, np.float32(0.0), entries)
    return entries.astype(ml_dtypes.bfloat16).astype(np.float32)


def band_x():
    m, i = np.arange(LANES)[:, None], np.arange(2 * NX)[None, :]
    return spectral_row(NX)[(m - i) % NX]


def band_y():
    depth = NY // N_COL
    r, s = np.arange(BAND)[:, None], np.arange(2 * PENCIL - BAND)[None, :] % PENCIL
    offset = (s // PIECE - r // PIECE) * depth + s % depth - r % depth
    same_level = (s % PIECE) // depth == (r % PIECE) // depth
    return np.where(same_level, spectral_row(NY)[offset % NY], np.float32(0.0))


def iota(shape, dim):
    return lax.broadcasted_iota(jnp.int32, shape, dim)


def split_points(points):
    line = ((points >> 9) * 43) >> 7
    tile = (points >> 7) - line * ROTOR_TILES
    return tile * ROTOR_LINES + line, points & (LANES - 1)


def kernel(
    fields, points, weights, turbines, counts, wide_x, wide_y,
    out, thrust_out,
    held, there, sent, back, stage_x, stage_y, tab_x, tab_y, advect, result,
    pts, wts, trb, cnt, sampled, picked, forced, push, own, from_row, from_y, from_z,
    local_sem, there_send, there_recv, back_send, back_recv, sum_send, sum_recv, out_sem,
):
    row = lax.axis_index("row")
    me = lax.axis_index("col")
    my_piece, my_half = me // 2, me % 2

    loads = [
        pltpu.make_async_copy(src, dst, local_sem.at[i])
        for i, (src, dst) in enumerate(
            [(fields, held), (points, pts), (weights, wts), (turbines, trb), (counts, cnt),
             (wide_x, stage_x), (wide_y, stage_y)]
        )
    ]

    barrier = pltpu.get_barrier_semaphore()

    def greet_col(k, carry):
        peer = lax.rem(me + k, N_COL)
        pl.semaphore_signal(barrier, inc=1, device_id={"col": peer}, device_id_type=MESH)
        return carry

    def greet_row(k, carry):
        peer = lax.rem(row + k, N_ROW)
        pl.semaphore_signal(barrier, inc=1, device_id={"row": peer}, device_id_type=MESH)
        return carry

    lax.fori_loop(1, N_COL, greet_col, 0)
    lax.fori_loop(1, N_ROW, greet_row, 0)
    for load in loads:
        load.start()
    pl.semaphore_wait(barrier, N_COL - 1 + N_ROW - 1)

    def field_piece(peer, chunk):
        start = pl.multiple_of((peer % 2) * HALF + chunk * CHUNK, CHUNK)
        return fields.at[pl.ds((peer // 2) * PIECE, PIECE), pl.ds(start, CHUNK)]

    for chunk in range(CHUNKS):

        def send_there(k, carry, chunk=chunk):
            peer = lax.rem(me + k, N_COL)
            pltpu.make_async_remote_copy(
                src_ref=field_piece(peer, chunk),
                dst_ref=there.at[chunk, pl.ds(me * PIECE, PIECE)],
                send_sem=there_send.at[chunk],
                recv_sem=there_recv.at[chunk],
                device_id={"col": peer},
                device_id_type=MESH,
            ).start()
            return carry

        lax.fori_loop(1, N_COL, send_there, 0)
        pltpu.make_async_copy(
            field_piece(me, chunk), there.at[chunk, pl.ds(me * PIECE, PIECE)], there_recv.at[chunk]
        ).start()

    for load in loads[:5]:
        load.wait()
    lines = held[0:ROTOR_LINES, :].astype(jnp.float32)
    tiles = [lines[:, LANES * i : LANES * (i + 1)] for i in range(ROTOR_TILES)]
    picked[...] = jnp.concatenate(tiles, axis=0).T.astype(jnp.bfloat16)
    table_rows = ROTOR_TILES * ROTOR_LINES

    def pick(group, carry):
        for i in range(4):
            b = group * 4 + i
            high, low = split_points(pts[pl.ds(b, 1), :])
            hot = (iota((table_rows, SAMPLES), 0) == high).astype(jnp.float32).astype(jnp.bfloat16)
            columns = jnp.dot(picked[...], hot, preferred_element_type=jnp.float32)
            chosen = jnp.where(iota((LANES, SAMPLES), 0) == low, columns, 0.0)
            sampled[pl.ds(b, 1), :] = jnp.sum(chosen, axis=0, keepdims=True)
        return carry

    lax.fori_loop(0, BLOCKS // 4, pick, 0)

    count_here = jnp.sum(
        jnp.where(iota((1, N_COL), 1) == me, cnt[...], 0), axis=1, keepdims=True
    )
    active = (iota((BLOCKS, 1), 0) < count_here).astype(jnp.float32)
    weight = wts[...].astype(jnp.float32) * active
    turbine_row = trb[pl.ds(me, 1), :]
    diagonal = iota((BLOCKS, BLOCKS), 0) == iota((BLOCKS, BLOCKS), 1)
    turbine = jnp.sum(jnp.where(diagonal, turbine_row, 0), axis=1, keepdims=True)
    belongs = (iota((BLOCKS, TURBINE_LANES), 1) == turbine).astype(jnp.float32)
    moments = (
        jnp.sum(weight * sampled[...], axis=1, keepdims=True),
        jnp.sum(weight, axis=1, keepdims=True),
    )
    per_moment = TURBINE_LANES // LANES
    for m in range(2):
        partial = jnp.sum(belongs * moments[m], axis=0, keepdims=True)
        for i in range(per_moment):
            at = m * per_moment + i
            own[0, at : at + 1, :] = partial[:, LANES * i : LANES * (i + 1)]

    def share(phase, peers, slots, peer_of):
        def send(k, carry):
            pltpu.make_async_remote_copy(
                src_ref=own.at[phase],
                dst_ref=slots.at[k - 1],
                send_sem=sum_send.at[phase],
                recv_sem=sum_recv.at[phase],
                device_id=peer_of(k),
                device_id_type=MESH,
            ).start()
            return carry

        lax.fori_loop(1, peers, send, 0)

    def collect(phase, slots):
        pltpu.make_async_copy(slots, slots, sum_recv.at[phase]).wait()
        pltpu.make_async_copy(slots, slots, sum_send.at[phase]).wait()
        return own[phase] + jnp.sum(slots[...], axis=0)

    z, y = me // RING_Y, me % RING_Y
    share(0, N_ROW, from_row, lambda k: {"row": lax.rem(row + k, N_ROW)})

    loads[5].wait()
    tab_x[...] = stage_x[...].astype(jnp.bfloat16)

    def along_x(i, carry):
        columns = pl.ds(pl.multiple_of(i * CHUNK, CHUNK), CHUNK)
        slices = [
            tab_x[:, pl.ds(pl.multiple_of(i * CHUNK + NX - LANES * a, LANES), CHUNK)]
            for a in range(NX // LANES)
        ]
        table = jnp.concatenate(slices, axis=0)
        speed = held[0:PLANE, columns].astype(jnp.float32)
        for f in range(FIELDS):
            lines = pl.ds(f * PLANE, PLANE)
            slope = jnp.dot(held[lines, :], table, preferred_element_type=jnp.float32)
            terms = -(speed * slope)
            if f == 2:
                heat = held[3 * PLANE : 4 * PLANE, columns].astype(jnp.float32)
                terms = terms + BUOYANCY * heat
            advect[lines, columns] = terms
        return carry

    lax.fori_loop(0, NX // CHUNK, along_x, 0)

    own[1] = collect(0, from_row)
    share(1, RING_Y, from_y, lambda k: {"col": z * RING_Y + lax.rem(y + k, RING_Y)})
    loads[6].wait()
    for i in range(8):
        lines = slice(i * PIECE, (i + 1) * PIECE)
        tab_y[lines, :] = stage_y[lines, :].astype(jnp.bfloat16)

    def along_y(chunk):
        pltpu.make_async_copy(there.at[chunk], there.at[chunk], there_recv.at[chunk]).wait()

        def tile(i, carry):
            start = pl.multiple_of(i * BAND, BAND)
            table = tab_y[:, pl.ds(pl.multiple_of((PENCIL - start) % PENCIL, BAND), PENCIL)]
            slope = jnp.dot(table, there[chunk], preferred_element_type=jnp.float32)
            sent[chunk, pl.ds(start, BAND), :] = slope.astype(jnp.bfloat16)
            return carry

        lax.fori_loop(0, PENCIL // BAND, tile, 0)
        landing = back.at[my_half, chunk, pl.ds(my_piece * PIECE, PIECE)]

        def send_back(k, carry):
            peer = lax.rem(me + k, N_COL)
            pltpu.make_async_remote_copy(
                src_ref=sent.at[chunk, pl.ds(peer * PIECE, PIECE)],
                dst_ref=landing,
                send_sem=back_send.at[chunk],
                recv_sem=back_recv.at[chunk],
                device_id={"col": peer},
                device_id_type=MESH,
            ).start()
            return carry

        lax.fori_loop(1, N_COL, send_back, 0)
        pltpu.make_async_copy(
            sent.at[chunk, pl.ds(me * PIECE, PIECE)], landing, back_recv.at[chunk]
        ).start()

    along_y(0)
    own[2] = collect(1, from_y)
    share(2, RING_Z, from_z, lambda k: {"col": lax.rem(z + k, RING_Z) * RING_Y + y})
    for chunk in range(1, CHUNKS):
        along_y(chunk)

    totals = collect(2, from_z)
    looked_up = []
    for m in range(2):
        parts = [totals[m * per_moment + i : m * per_moment + i + 1, :] for i in range(per_moment)]
        found = belongs * jnp.concatenate(parts, axis=1)
        looked_up.append(jnp.sum(found, axis=1, keepdims=True))
    disk_speed = looked_up[0] / (looked_up[1] + 1.0 - active)
    push[...] = -CT_HALF * (disk_speed * jnp.abs(disk_speed)) * weight
    thrust_copy = pltpu.make_async_copy(push, thrust_out, out_sem.at[2 * CHUNKS])
    thrust_copy.start()
    forced[...] = jnp.zeros_like(forced)

    def spread(group, carry):
        total = forced[...]
        for i in range(2):
            b = group * 2 + i
            high, low = split_points(pts[pl.ds(b, 1), :])
            hot = (iota((table_rows, SAMPLES), 0) == high).astype(jnp.float32).astype(jnp.bfloat16)
            value = push[pl.ds(b, 1), :]
            upper = value.astype(jnp.bfloat16).astype(jnp.float32)
            here = iota((LANES, SAMPLES), 0) == low
            placed = jnp.concatenate(
                [jnp.where(here, upper, 0.0), jnp.where(here, value - upper, 0.0)], axis=0
            ).astype(jnp.bfloat16)
            total = total + lax.dot_general(
                hot, placed, (((1,), (1,)), ((), ())), preferred_element_type=jnp.float32
            )
        forced[...] = total
        return carry

    lax.fori_loop(0, BLOCKS // 2, spread, 0)
    for i in range(ROTOR_TILES):
        lines = slice(i * ROTOR_LINES, (i + 1) * ROTOR_LINES)
        columns = slice(i * LANES, (i + 1) * LANES)
        advect[0:ROTOR_LINES, columns] += forced[lines, :LANES] + forced[lines, LANES:]

    stores = []
    for chunk in range(CHUNKS):
        pltpu.make_async_copy(back.at[:, chunk], back.at[:, chunk], back_recv.at[chunk]).wait()
        for half in range(2):
            columns = pl.ds(half * HALF + chunk * CHUNK, CHUNK)
            across = held[PLANE : 2 * PLANE, columns].astype(jnp.float32)
            for f in range(FIELDS):
                lines = pl.ds(f * PLANE, PLANE)
                term = across * back[half, chunk, lines, :].astype(jnp.float32)
                result[lines, columns] = (advect[lines, columns] - term).astype(jnp.bfloat16)
            store = pltpu.make_async_copy(
                result.at[:, columns], out.at[:, columns], out_sem.at[2 * chunk + half]
            )
            store.start()
            stores.append(store)

    for chunk in range(CHUNKS):
        others = pl.ds(0, PENCIL - PIECE)
        pltpu.make_async_copy(
            there.at[chunk, others], there.at[chunk, others], there_send.at[chunk]
        ).wait()
        pltpu.make_async_copy(
            sent.at[chunk, others], sent.at[chunk, others], back_send.at[chunk]
        ).wait()
    for store in stores:
        store.wait()
    thrust_copy.wait()


def per_device(fields, block_points, sample_weight, block_turbine, block_count):
    bf16, f32, i32 = jnp.bfloat16, jnp.float32, jnp.int32
    dma = pltpu.SemaphoreType.DMA
    tendency, thrust = pl.pallas_call(
        kernel,
        out_shape=(
            jax.ShapeDtypeStruct((ROWS, NX), bf16),
            jax.ShapeDtypeStruct((BLOCKS, SAMPLES), f32),
        ),
        in_specs=[HBM] * 7,
        out_specs=(HBM, HBM),
        scratch_shapes=[
            pltpu.VMEM((ROWS, NX), bf16),
            pltpu.VMEM((CHUNKS, PENCIL, CHUNK), bf16),
            pltpu.VMEM((CHUNKS, PENCIL, CHUNK), bf16),
            pltpu.VMEM((2, CHUNKS, ROWS, CHUNK), bf16),
            pltpu.VMEM((LANES, 2 * NX), f32),
            pltpu.VMEM((BAND, 2 * PENCIL - BAND), f32),
            pltpu.VMEM((LANES, 2 * NX), bf16),
            pltpu.VMEM((BAND, 2 * PENCIL - BAND), bf16),
            pltpu.VMEM((ROWS, NX), f32),
            pltpu.VMEM((ROWS, NX), bf16),
            pltpu.VMEM((BLOCKS, SAMPLES), i32),
            pltpu.VMEM((BLOCKS, SAMPLES), bf16),
            pltpu.VMEM((N_COL, BLOCKS), i32),
            pltpu.VMEM((1, N_COL), i32),
            pltpu.VMEM((BLOCKS, SAMPLES), f32),
            pltpu.VMEM((LANES, ROTOR_TILES * ROTOR_LINES), bf16),
            pltpu.VMEM((ROTOR_TILES * ROTOR_LINES, 2 * LANES), f32),
            pltpu.VMEM((BLOCKS, SAMPLES), f32),
            pltpu.VMEM((3, 8, LANES), f32),
            pltpu.VMEM((N_ROW - 1, 8, LANES), f32),
            pltpu.VMEM((RING_Y - 1, 8, LANES), f32),
            pltpu.VMEM((RING_Z - 1, 8, LANES), f32),
            dma((7,)),
            dma((CHUNKS,)),
            dma((CHUNKS,)),
            dma((CHUNKS,)),
            dma((CHUNKS,)),
            dma((3,)),
            dma((3,)),
            dma((2 * CHUNKS + 1,)),
        ],
        compiler_params=pltpu.CompilerParams(
            collective_id=0, has_side_effects=True, vmem_limit_bytes=56 * 2**20
        ),
        name="advection",
    )(
        fields.reshape(ROWS, NX),
        block_points.reshape(BLOCKS, SAMPLES),
        sample_weight.reshape(BLOCKS, SAMPLES),
        block_turbine.reshape(N_COL, BLOCKS),
        block_count,
        jnp.asarray(band_x()),
        jnp.asarray(band_y()),
    )
    return tendency.reshape(fields.shape), thrust.reshape(block_points.shape)


def solution(mesh):
    placed = (
        P(None, "row", "col", None),
        P("row", "col", None, None),
        P("row", "col", None, None),
        P("row", None, None),
        P("row", None),
    )
    return jax.shard_map(
        per_device,
        mesh=mesh,
        in_specs=placed,
        out_specs=(P(None, "row", "col", None), P("row", "col", None, None)),
        check_vma=False,
    )
```

```python
import functools

import jax
import jax.numpy as jnp
import ml_dtypes
import numpy as np
from jax import lax
from jax.experimental import pallas as pl
from jax.experimental.pallas import tpu as pltpu
from jax.sharding import PartitionSpec as P

MESH = pl.DeviceIdType.MESH
HBM = pl.BlockSpec(memory_space=pltpu.HBM)
VMEM = pl.BlockSpec(memory_space=pltpu.VMEM)

N_ROW = 8
N_COL = 32
RING_Y = 4
RING_Z = 8
FIELDS = 4
NX = 1536
NY = 768
TURBINES = 400
BLOCKS = 48
SAMPLES = 256
LANES = 128
CT_HALF = 2.0 / 3.0
BUOYANCY = 0.3

ROWS = 768
PLANE = ROWS // FIELDS
PIECE = 2 * ROWS // N_COL
HALF = NX // 2
CHUNK = 256
CHUNKS = HALF // CHUNK
PENCIL = N_COL * PIECE
ROTOR_LINES = 16
ROTOR_TILES = NX // LANES
TURBINE_LANES = 512
BAND = 8 * PIECE


def spectral_row(length):
    offset = np.arange(length, dtype=np.int32)
    phase_angle = offset.astype(np.float32) * np.float32(np.pi / length)
    parity = np.float32(1.0) - np.float32(2.0) * (offset % 2).astype(np.float32)
    sine_safe = np.where(offset == 0, np.float32(1.0), np.sin(phase_angle))
    entries = np.float32(-(np.pi / length)) * parity * np.cos(phase_angle) / sine_safe
    entries = np.where(offset == 0, np.float32(0.0), entries)
    return entries.astype(ml_dtypes.bfloat16).astype(np.float32)


def band_x():
    m, i = np.arange(LANES)[:, None], np.arange(2 * NX)[None, :]
    return spectral_row(NX)[(m - i) % NX]


def band_y():
    depth = NY // N_COL
    r, s = np.arange(BAND)[:, None], np.arange(2 * PENCIL - BAND)[None, :] % PENCIL
    offset = (s // PIECE - r // PIECE) * depth + s % depth - r % depth
    same_level = (s % PIECE) // depth == (r % PIECE) // depth
    return np.where(same_level, spectral_row(NY)[offset % NY], np.float32(0.0))


def iota(shape, dim):
    return lax.broadcasted_iota(jnp.int32, shape, dim)


def split_points(points):
    line = ((points >> 9) * 43) >> 7
    tile = (points >> 7) - line * ROTOR_TILES
    return tile * ROTOR_LINES + line, points & (LANES - 1)


def kernel(
    fields, points, weights, turbines, counts, wide_x, wide_y,
    held, last_back, advect, result, push,
    there, sent, back, stage_x, stage_y, tab_x, tab_y,
    pts, wts, trb, cnt, sampled, picked, forced, own, from_row, from_y, from_z,
    local_sem, there_send, there_recv, back_send, back_recv, sum_send, sum_recv,
):
    row = lax.axis_index("row")
    me = lax.axis_index("col")
    my_piece, my_half = me // 2, me % 2

    loads = [
        pltpu.make_async_copy(src, dst, local_sem.at[i])
        for i, (src, dst) in enumerate(
            [(fields, held), (points, pts), (weights, wts), (turbines, trb), (counts, cnt),
             (wide_x, stage_x), (wide_y, stage_y)]
        )
    ]

    barrier = pltpu.get_barrier_semaphore()

    def greet_col(k, carry):
        peer = lax.rem(me + k, N_COL)
        pl.semaphore_signal(barrier, inc=1, device_id={"col": peer}, device_id_type=MESH)
        return carry

    def greet_row(k, carry):
        peer = lax.rem(row + k, N_ROW)
        pl.semaphore_signal(barrier, inc=1, device_id={"row": peer}, device_id_type=MESH)
        return carry

    lax.fori_loop(1, N_COL, greet_col, 0)
    lax.fori_loop(1, N_ROW, greet_row, 0)
    for load in loads:
        load.start()
    pl.semaphore_wait(barrier, N_COL - 1 + N_ROW - 1)

    def field_piece(peer, chunk):
        start = pl.multiple_of((peer % 2) * HALF + chunk * CHUNK, CHUNK)
        return fields.at[pl.ds((peer // 2) * PIECE, PIECE), pl.ds(start, CHUNK)]

    for chunk in range(CHUNKS):

        def send_there(k, carry, chunk=chunk):
            peer = lax.rem(me + k, N_COL)
            pltpu.make_async_remote_copy(
                src_ref=field_piece(peer, chunk),
                dst_ref=there.at[chunk, pl.ds(me * PIECE, PIECE)],
                send_sem=there_send.at[chunk],
                recv_sem=there_recv.at[chunk],
                device_id={"col": peer},
                device_id_type=MESH,
            ).start()
            return carry

        lax.fori_loop(1, N_COL, send_there, 0)
        pltpu.make_async_copy(
            field_piece(me, chunk), there.at[chunk, pl.ds(me * PIECE, PIECE)], there_recv.at[chunk]
        ).start()

    for load in loads[:5]:
        load.wait()
    lines = held[0:ROTOR_LINES, :].astype(jnp.float32)
    tiles = [lines[:, LANES * i : LANES * (i + 1)] for i in range(ROTOR_TILES)]
    picked[...] = jnp.concatenate(tiles, axis=0).T.astype(jnp.bfloat16)
    table_rows = ROTOR_TILES * ROTOR_LINES

    def pick(group, carry):
        for i in range(4):
            b = group * 4 + i
            high, low = split_points(pts[pl.ds(b, 1), :])
            hot = (iota((table_rows, SAMPLES), 0) == high).astype(jnp.float32).astype(jnp.bfloat16)
            columns = jnp.dot(picked[...], hot, preferred_element_type=jnp.float32)
            chosen = jnp.where(iota((LANES, SAMPLES), 0) == low, columns, 0.0)
            sampled[pl.ds(b, 1), :] = jnp.sum(chosen, axis=0, keepdims=True)
        return carry

    lax.fori_loop(0, BLOCKS // 4, pick, 0)

    count_here = jnp.sum(
        jnp.where(iota((1, N_COL), 1) == me, cnt[...], 0), axis=1, keepdims=True
    )
    active = (iota((BLOCKS, 1), 0) < count_here).astype(jnp.float32)
    weight = wts[...].astype(jnp.float32) * active
    turbine_row = trb[pl.ds(me, 1), :]
    diagonal = iota((BLOCKS, BLOCKS), 0) == iota((BLOCKS, BLOCKS), 1)
    turbine = jnp.sum(jnp.where(diagonal, turbine_row, 0), axis=1, keepdims=True)
    belongs = (iota((BLOCKS, TURBINE_LANES), 1) == turbine).astype(jnp.float32)
    moments = (
        jnp.sum(weight * sampled[...], axis=1, keepdims=True),
        jnp.sum(weight, axis=1, keepdims=True),
    )
    per_moment = TURBINE_LANES // LANES
    for m in range(2):
        partial = jnp.sum(belongs * moments[m], axis=0, keepdims=True)
        for i in range(per_moment):
            at = m * per_moment + i
            own[0, at : at + 1, :] = partial[:, LANES * i : LANES * (i + 1)]

    def share(phase, peers, slots, peer_of):
        def send(k, carry):
            pltpu.make_async_remote_copy(
                src_ref=own.at[phase],
                dst_ref=slots.at[k - 1],
                send_sem=sum_send.at[phase],
                recv_sem=sum_recv.at[phase],
                device_id=peer_of(k),
                device_id_type=MESH,
            ).start()
            return carry

        lax.fori_loop(1, peers, send, 0)

    def collect(phase, slots):
        pltpu.make_async_copy(slots, slots, sum_recv.at[phase]).wait()
        pltpu.make_async_copy(slots, slots, sum_send.at[phase]).wait()
        return own[phase] + jnp.sum(slots[...], axis=0)

    z, y = me // RING_Y, me % RING_Y
    share(0, N_ROW, from_row, lambda k: {"row": lax.rem(row + k, N_ROW)})

    loads[5].wait()
    tab_x[...] = stage_x[...].astype(jnp.bfloat16)

    def along_x(i, carry):
        columns = pl.ds(pl.multiple_of(i * CHUNK, CHUNK), CHUNK)
        slices = [
            tab_x[:, pl.ds(pl.multiple_of(i * CHUNK + NX - LANES * a, LANES), CHUNK)]
            for a in range(NX // LANES)
        ]
        table = jnp.concatenate(slices, axis=0)
        speed = held[0:PLANE, columns].astype(jnp.float32)
        for f in range(FIELDS):
            lines = pl.ds(f * PLANE, PLANE)
            slope = jnp.dot(held[lines, :], table, preferred_element_type=jnp.float32)
            terms = -(speed * slope)
            if f == 2:
                heat = held[3 * PLANE : 4 * PLANE, columns].astype(jnp.float32)
                terms = terms + BUOYANCY * heat
            advect[lines, columns] = terms
        return carry

    lax.fori_loop(0, NX // CHUNK, along_x, 0)

    own[1] = collect(0, from_row)
    share(1, RING_Y, from_y, lambda k: {"col": z * RING_Y + lax.rem(y + k, RING_Y)})
    loads[6].wait()
    for i in range(8):
        lines = slice(i * PIECE, (i + 1) * PIECE)
        tab_y[lines, :] = stage_y[lines, :].astype(jnp.bfloat16)

    def along_y(chunk):
        pltpu.make_async_copy(there.at[chunk], there.at[chunk], there_recv.at[chunk]).wait()

        def tile(i, carry):
            start = pl.multiple_of(i * BAND, BAND)
            table = tab_y[:, pl.ds(pl.multiple_of((PENCIL - start) % PENCIL, BAND), PENCIL)]
            slope = jnp.dot(table, there[chunk], preferred_element_type=jnp.float32)
            sent[chunk, pl.ds(start, BAND), :] = slope.astype(jnp.bfloat16)
            return carry

        lax.fori_loop(0, PENCIL // BAND, tile, 0)
        lines = pl.ds(my_piece * PIECE, PIECE)
        if chunk < CHUNKS - 1:
            landing = back.at[my_half, chunk, lines]
        else:
            landing = last_back.at[my_half, lines]

        def send_back(k, carry):
            peer = lax.rem(me + k, N_COL)
            pltpu.make_async_remote_copy(
                src_ref=sent.at[chunk, pl.ds(peer * PIECE, PIECE)],
                dst_ref=landing,
                send_sem=back_send.at[chunk],
                recv_sem=back_recv.at[chunk],
                device_id={"col": peer},
                device_id_type=MESH,
            ).start()
            return carry

        lax.fori_loop(1, N_COL, send_back, 0)
        pltpu.make_async_copy(
            sent.at[chunk, pl.ds(me * PIECE, PIECE)], landing, back_recv.at[chunk]
        ).start()

    along_y(0)
    own[2] = collect(1, from_y)
    share(2, RING_Z, from_z, lambda k: {"col": lax.rem(z + k, RING_Z) * RING_Y + y})
    for chunk in range(1, CHUNKS):
        along_y(chunk)

    totals = collect(2, from_z)
    looked_up = []
    for m in range(2):
        parts = [totals[m * per_moment + i : m * per_moment + i + 1, :] for i in range(per_moment)]
        found = belongs * jnp.concatenate(parts, axis=1)
        looked_up.append(jnp.sum(found, axis=1, keepdims=True))
    disk_speed = looked_up[0] / (looked_up[1] + 1.0 - active)
    push[...] = -CT_HALF * (disk_speed * jnp.abs(disk_speed)) * weight
    forced[...] = jnp.zeros_like(forced)

    def spread(group, carry):
        total = forced[...]
        for i in range(2):
            b = group * 2 + i
            high, low = split_points(pts[pl.ds(b, 1), :])
            hot = (iota((table_rows, SAMPLES), 0) == high).astype(jnp.float32).astype(jnp.bfloat16)
            value = push[pl.ds(b, 1), :]
            upper = value.astype(jnp.bfloat16).astype(jnp.float32)
            here = iota((LANES, SAMPLES), 0) == low
            placed = jnp.concatenate(
                [jnp.where(here, upper, 0.0), jnp.where(here, value - upper, 0.0)], axis=0
            ).astype(jnp.bfloat16)
            total = total + lax.dot_general(
                hot, placed, (((1,), (1,)), ((), ())), preferred_element_type=jnp.float32
            )
        forced[...] = total
        return carry

    lax.fori_loop(0, BLOCKS // 2, spread, 0)
    for i in range(ROTOR_TILES):
        lines = slice(i * ROTOR_LINES, (i + 1) * ROTOR_LINES)
        columns = slice(i * LANES, (i + 1) * LANES)
        advect[0:ROTOR_LINES, columns] += forced[lines, :LANES] + forced[lines, LANES:]

    for chunk in range(CHUNKS):
        arrived = back.at[:, chunk] if chunk < CHUNKS - 1 else last_back
        pltpu.make_async_copy(arrived, arrived, back_recv.at[chunk]).wait()
        if chunk < CHUNKS - 1:
            for half in range(2):
                combine(held, arrived.at[half], advect, result, chunk, half)

    for chunk in range(CHUNKS):
        others = pl.ds(0, PENCIL - PIECE)
        pltpu.make_async_copy(
            there.at[chunk, others], there.at[chunk, others], there_send.at[chunk]
        ).wait()
        pltpu.make_async_copy(
            sent.at[chunk, others], sent.at[chunk, others], back_send.at[chunk]
        ).wait()


def combine(held, arrived, advect, result, chunk, half):
    columns = pl.ds(half * HALF + chunk * CHUNK, CHUNK)
    across = held[PLANE : 2 * PLANE, columns].astype(jnp.float32)
    for f in range(FIELDS):
        lines = pl.ds(f * PLANE, PLANE)
        term = across * arrived[lines, :].astype(jnp.float32)
        result[lines, columns] = (advect[lines, columns] - term).astype(jnp.bfloat16)


def finish(held, last_back, advect, result, push, out, thrust_out, merged, out_sem):
    stores = [pltpu.make_async_copy(push, thrust_out, out_sem.at[0])]
    for half in range(2):
        early = pl.ds(half * HALF, HALF - CHUNK)
        stores.append(
            pltpu.make_async_copy(result.at[:, early], out.at[:, early], out_sem.at[1 + half])
        )
    for store in stores:
        store.start()
    for half in range(2):
        combine(held, last_back.at[half], advect, merged, CHUNKS - 1, half)
        late = pl.ds((half + 1) * HALF - CHUNK, CHUNK)
        stores.append(
            pltpu.make_async_copy(merged.at[:, late], out.at[:, late], out_sem.at[3 + half])
        )
        stores[-1].start()
    for store in stores:
        store.wait()


def per_device(fields, block_points, sample_weight, block_turbine, block_count):
    bf16, f32, i32 = jnp.bfloat16, jnp.float32, jnp.int32
    dma = pltpu.SemaphoreType.DMA
    parts = pl.pallas_call(
        kernel,
        out_shape=(
            pltpu.VMEM((ROWS, NX), bf16),
            pltpu.VMEM((2, ROWS, CHUNK), bf16),
            pltpu.VMEM((ROWS, NX), f32),
            pltpu.VMEM((ROWS, NX), bf16),
            pltpu.VMEM((BLOCKS, SAMPLES), f32),
        ),
        in_specs=[HBM] * 7,
        out_specs=(VMEM,) * 5,
        scratch_shapes=[
            pltpu.VMEM((CHUNKS, PENCIL, CHUNK), bf16),
            pltpu.VMEM((CHUNKS, PENCIL, CHUNK), bf16),
            pltpu.VMEM((2, CHUNKS - 1, ROWS, CHUNK), bf16),
            pltpu.VMEM((LANES, 2 * NX), f32),
            pltpu.VMEM((BAND, 2 * PENCIL - BAND), f32),
            pltpu.VMEM((LANES, 2 * NX), bf16),
            pltpu.VMEM((BAND, 2 * PENCIL - BAND), bf16),
            pltpu.VMEM((BLOCKS, SAMPLES), i32),
            pltpu.VMEM((BLOCKS, SAMPLES), bf16),
            pltpu.VMEM((N_COL, BLOCKS), i32),
            pltpu.VMEM((1, N_COL), i32),
            pltpu.VMEM((BLOCKS, SAMPLES), f32),
            pltpu.VMEM((LANES, ROTOR_TILES * ROTOR_LINES), bf16),
            pltpu.VMEM((ROTOR_TILES * ROTOR_LINES, 2 * LANES), f32),
            pltpu.VMEM((3, 8, LANES), f32),
            pltpu.VMEM((N_ROW - 1, 8, LANES), f32),
            pltpu.VMEM((RING_Y - 1, 8, LANES), f32),
            pltpu.VMEM((RING_Z - 1, 8, LANES), f32),
            dma((7,)),
            dma((CHUNKS,)),
            dma((CHUNKS,)),
            dma((CHUNKS,)),
            dma((CHUNKS,)),
            dma((3,)),
            dma((3,)),
        ],
        compiler_params=pltpu.CompilerParams(
            collective_id=0, has_side_effects=True, vmem_limit_bytes=50 * 2**20
        ),
        name="advection",
    )(
        fields.reshape(ROWS, NX),
        block_points.reshape(BLOCKS, SAMPLES),
        sample_weight.reshape(BLOCKS, SAMPLES),
        block_turbine.reshape(N_COL, BLOCKS),
        block_count,
        jnp.asarray(band_x()),
        jnp.asarray(band_y()),
    )
    tendency, thrust = pl.pallas_call(
        finish,
        out_shape=(
            jax.ShapeDtypeStruct((ROWS, NX), bf16),
            jax.ShapeDtypeStruct((BLOCKS, SAMPLES), f32),
        ),
        in_specs=[VMEM] * 5,
        out_specs=(HBM, HBM),
        scratch_shapes=[pltpu.VMEM((ROWS, NX), bf16), dma((5,))],
        compiler_params=pltpu.CompilerParams(vmem_limit_bytes=16 * 2**20),
        name="finish",
    )(*parts)
    return tendency.reshape(fields.shape), thrust.reshape(block_points.shape)


def solution(mesh):
    placed = (
        P(None, "row", "col", None),
        P("row", "col", None, None),
        P("row", "col", None, None),
        P("row", None, None),
        P("row", None),
    )
    return jax.shard_map(
        per_device,
        mesh=mesh,
        in_specs=placed,
        out_specs=(P(None, "row", "col", None), P("row", "col", None, None)),
        check_vma=False,
    )
```

```python
import functools

import jax
import jax.numpy as jnp
import ml_dtypes
import numpy as np
from jax import lax
from jax.experimental import pallas as pl
from jax.experimental.pallas import tpu as pltpu
from jax.sharding import PartitionSpec as P

MESH = pl.DeviceIdType.MESH
HBM = pl.BlockSpec(memory_space=pltpu.HBM)
VMEM = pl.BlockSpec(memory_space=pltpu.VMEM)

N_ROW = 8
N_COL = 32
RING_Y = 4
RING_Z = 8
FIELDS = 4
NX = 1536
NY = 768
TURBINES = 400
BLOCKS = 48
SAMPLES = 256
LANES = 128
CT_HALF = 2.0 / 3.0
BUOYANCY = 0.3

ROWS = 768
PLANE = ROWS // FIELDS
PIECE = 2 * ROWS // N_COL
HALF = NX // 2
CHUNK = 256
CHUNKS = HALF // CHUNK
PENCIL = N_COL * PIECE
ROTOR_LINES = 16
ROTOR_TILES = NX // LANES
TURBINE_LANES = 512
BAND = 8 * PIECE


def spectral_row(length):
    offset = np.arange(length, dtype=np.int32)
    phase_angle = offset.astype(np.float32) * np.float32(np.pi / length)
    parity = np.float32(1.0) - np.float32(2.0) * (offset % 2).astype(np.float32)
    sine_safe = np.where(offset == 0, np.float32(1.0), np.sin(phase_angle))
    entries = np.float32(-(np.pi / length)) * parity * np.cos(phase_angle) / sine_safe
    entries = np.where(offset == 0, np.float32(0.0), entries)
    return entries.astype(ml_dtypes.bfloat16).astype(np.float32)


def band_x():
    m, i = np.arange(LANES)[:, None], np.arange(2 * NX)[None, :]
    return spectral_row(NX)[(m - i) % NX]


def band_y():
    depth = NY // N_COL
    r, s = np.arange(BAND)[:, None], np.arange(2 * PENCIL - BAND)[None, :] % PENCIL
    offset = (s // PIECE - r // PIECE) * depth + s % depth - r % depth
    same_level = (s % PIECE) // depth == (r % PIECE) // depth
    return np.where(same_level, spectral_row(NY)[offset % NY], np.float32(0.0))


def alternating(i):
    return lax.rem(jnp.where(i % 2 == 1, (i + 1) // 2, RING_Z - i // 2), RING_Z)


def iota(shape, dim):
    return lax.broadcasted_iota(jnp.int32, shape, dim)


def split_points(points):
    line = ((points >> 9) * 43) >> 7
    tile = (points >> 7) - line * ROTOR_TILES
    return tile * ROTOR_LINES + line, points & (LANES - 1)


def kernel(
    fields, points, weights, turbines, counts, wide_x, wide_y,
    held, last_back, advect, result, push,
    there, sent, back, stage_x, stage_y, tab_x, tab_y,
    pts, wts, trb, cnt, sampled, picked, forced, own, from_row, from_y, from_z,
    local_sem, known, there_send, there_recv, back_send, back_recv, sum_send, sum_recv,
):
    row = lax.axis_index("row")
    me = lax.axis_index("col")
    my_piece, my_half = me // 2, me % 2

    loads = [
        pltpu.make_async_copy(src, dst, local_sem.at[i])
        for i, (src, dst) in enumerate(
            [(fields, held), (points, pts), (weights, wts), (turbines, trb), (counts, cnt),
             (wide_x, stage_x), (wide_y, stage_y)]
        )
    ]

    z, y = me // RING_Y, me % RING_Y

    def col_at(step_z, step_y):
        return lax.rem(z + step_z, RING_Z) * RING_Y + lax.rem(y + step_y, RING_Y)

    def greet(semaphore, steps):
        for step in steps:
            pl.semaphore_signal(
                semaphore, inc=1, device_id={"col": col_at(*step)}, device_id_type=MESH
            )

    def greet_row(k, carry):
        peer = lax.rem(row + k, N_ROW)
        pl.semaphore_signal(barrier, inc=1, device_id={"row": peer}, device_id_type=MESH)
        return carry

    def field_piece(peer, chunk):
        start = pl.multiple_of((peer % 2) * HALF + chunk * CHUNK, CHUNK)
        return fields.at[pl.ds((peer // 2) * PIECE, PIECE), pl.ds(start, CHUNK)]

    def send_there(peer, chunk):
        pltpu.make_async_remote_copy(
            src_ref=field_piece(peer, chunk),
            dst_ref=there.at[chunk, pl.ds(me * PIECE, PIECE)],
            send_sem=there_send.at[chunk],
            recv_sem=there_recv.at[chunk],
            device_id={"col": peer},
            device_id_type=MESH,
        ).start()

    barrier = pltpu.get_barrier_semaphore()
    beside = ((1, 0), (7, 0), (0, 1), (0, 3))
    greet(barrier, beside)
    lax.fori_loop(1, N_ROW, greet_row, 0)
    for load in loads:
        load.start()
    pl.semaphore_wait(barrier, len(beside) + N_ROW - 1)
    greet(known.at[0], beside)
    for step in beside:
        for chunk in range(CHUNKS):
            send_there(col_at(*step), chunk)
    pl.semaphore_wait(known.at[0], len(beside))
    two_away = ((2, 0), (6, 0), (0, 2))
    greet(known.at[1], two_away)
    for step in two_away + ((1, 1), (1, 3), (7, 1), (7, 3)):
        for chunk in range(CHUNKS):
            send_there(col_at(*step), chunk)
    pl.semaphore_wait(known.at[1], len(two_away))
    greet(known.at[2], two_away[:2])
    pl.semaphore_wait(known.at[2], 2)
    for chunk in range(CHUNKS):

        def send_far(i, carry, chunk=chunk):
            far = i // RING_Y
            send_there(col_at(jnp.where(far == 0, 4, 1 + 2 * far), i % RING_Y), chunk)
            return carry

        def send_middle(i, carry, chunk=chunk):
            send_there(col_at(2 + 4 * (i // 3), 1 + i % 3), chunk)
            return carry

        lax.fori_loop(0, 3 * RING_Y, send_far, 0)
        lax.fori_loop(0, 6, send_middle, 0)
        for step in ((1, 2), (7, 2)):
            send_there(col_at(*step), chunk)
        pltpu.make_async_copy(
            field_piece(me, chunk), there.at[chunk, pl.ds(me * PIECE, PIECE)], there_recv.at[chunk]
        ).start()

    for load in loads[:5]:
        load.wait()
    lines = held[0:ROTOR_LINES, :].astype(jnp.float32)
    tiles = [lines[:, LANES * i : LANES * (i + 1)] for i in range(ROTOR_TILES)]
    picked[...] = jnp.concatenate(tiles, axis=0).T.astype(jnp.bfloat16)
    table_rows = ROTOR_TILES * ROTOR_LINES

    def pick(group, carry):
        for i in range(4):
            b = group * 4 + i
            high, low = split_points(pts[pl.ds(b, 1), :])
            hot = (iota((table_rows, SAMPLES), 0) == high).astype(jnp.float32).astype(jnp.bfloat16)
            columns = jnp.dot(picked[...], hot, preferred_element_type=jnp.float32)
            chosen = jnp.where(iota((LANES, SAMPLES), 0) == low, columns, 0.0)
            sampled[pl.ds(b, 1), :] = jnp.sum(chosen, axis=0, keepdims=True)
        return carry

    lax.fori_loop(0, BLOCKS // 4, pick, 0)

    count_here = jnp.sum(
        jnp.where(iota((1, N_COL), 1) == me, cnt[...], 0), axis=1, keepdims=True
    )
    active = (iota((BLOCKS, 1), 0) < count_here).astype(jnp.float32)
    weight = wts[...].astype(jnp.float32) * active
    turbine_row = trb[pl.ds(me, 1), :]
    diagonal = iota((BLOCKS, BLOCKS), 0) == iota((BLOCKS, BLOCKS), 1)
    turbine = jnp.sum(jnp.where(diagonal, turbine_row, 0), axis=1, keepdims=True)
    belongs = (iota((BLOCKS, TURBINE_LANES), 1) == turbine).astype(jnp.float32)
    moments = (
        jnp.sum(weight * sampled[...], axis=1, keepdims=True),
        jnp.sum(weight, axis=1, keepdims=True),
    )
    per_moment = TURBINE_LANES // LANES
    for m in range(2):
        partial = jnp.sum(belongs * moments[m], axis=0, keepdims=True)
        for i in range(per_moment):
            at = m * per_moment + i
            own[0, at : at + 1, :] = partial[:, LANES * i : LANES * (i + 1)]

    def share(phase, peers, slots, peer_of):
        def send(k, carry):
            pltpu.make_async_remote_copy(
                src_ref=own.at[phase],
                dst_ref=slots.at[k - 1],
                send_sem=sum_send.at[phase],
                recv_sem=sum_recv.at[phase],
                device_id=peer_of(k),
                device_id_type=MESH,
            ).start()
            return carry

        lax.fori_loop(1, peers, send, 0)

    def collect(phase, slots):
        pltpu.make_async_copy(slots, slots, sum_recv.at[phase]).wait()
        pltpu.make_async_copy(slots, slots, sum_send.at[phase]).wait()
        return own[phase] + jnp.sum(slots[...], axis=0)

    share(0, N_ROW, from_row, lambda k: {"row": lax.rem(row + k, N_ROW)})

    loads[5].wait()
    tab_x[...] = stage_x[...].astype(jnp.bfloat16)

    def along_x(i, carry):
        columns = pl.ds(pl.multiple_of(i * CHUNK, CHUNK), CHUNK)
        slices = [
            tab_x[:, pl.ds(pl.multiple_of(i * CHUNK + NX - LANES * a, LANES), CHUNK)]
            for a in range(NX // LANES)
        ]
        table = jnp.concatenate(slices, axis=0)
        speed = held[0:PLANE, columns].astype(jnp.float32)
        for f in range(FIELDS):
            lines = pl.ds(f * PLANE, PLANE)
            slope = jnp.dot(held[lines, :], table, preferred_element_type=jnp.float32)
            terms = -(speed * slope)
            if f == 2:
                heat = held[3 * PLANE : 4 * PLANE, columns].astype(jnp.float32)
                terms = terms + BUOYANCY * heat
            advect[lines, columns] = terms
        return carry

    lax.fori_loop(0, NX // CHUNK, along_x, 0)

    own[1] = collect(0, from_row)
    share(1, RING_Y, from_y, lambda k: {"col": z * RING_Y + lax.rem(y + k, RING_Y)})
    loads[6].wait()
    for i in range(8):
        lines = slice(i * PIECE, (i + 1) * PIECE)
        tab_y[lines, :] = stage_y[lines, :].astype(jnp.bfloat16)

    def along_y(chunk):
        pltpu.make_async_copy(there.at[chunk], there.at[chunk], there_recv.at[chunk]).wait()

        def tile(i, carry):
            start = pl.multiple_of(i * BAND, BAND)
            table = tab_y[:, pl.ds(pl.multiple_of((PENCIL - start) % PENCIL, BAND), PENCIL)]
            slope = jnp.dot(table, there[chunk], preferred_element_type=jnp.float32)
            sent[chunk, pl.ds(start, BAND), :] = slope.astype(jnp.bfloat16)
            return carry

        lax.fori_loop(0, PENCIL // BAND, tile, 0)
        lines = pl.ds(my_piece * PIECE, PIECE)
        if chunk < CHUNKS - 1:
            landing = back.at[my_half, chunk, lines]
        else:
            landing = last_back.at[my_half, lines]

        def send_back(k, carry):
            peer = k - 1 + (k - 1 >= me).astype(jnp.int32)
            pltpu.make_async_remote_copy(
                src_ref=sent.at[chunk, pl.ds(peer * PIECE, PIECE)],
                dst_ref=landing,
                send_sem=back_send.at[chunk],
                recv_sem=back_recv.at[chunk],
                device_id={"col": peer},
                device_id_type=MESH,
            ).start()
            return carry

        lax.fori_loop(1, N_COL, send_back, 0)
        pltpu.make_async_copy(
            sent.at[chunk, pl.ds(me * PIECE, PIECE)], landing, back_recv.at[chunk]
        ).start()

    along_y(0)
    own[2] = collect(1, from_y)
    share(2, RING_Z, from_z, lambda k: {"col": lax.rem(z + k, RING_Z) * RING_Y + y})
    for chunk in range(1, CHUNKS):
        along_y(chunk)

    totals = collect(2, from_z)
    looked_up = []
    for m in range(2):
        parts = [totals[m * per_moment + i : m * per_moment + i + 1, :] for i in range(per_moment)]
        found = belongs * jnp.concatenate(parts, axis=1)
        looked_up.append(jnp.sum(found, axis=1, keepdims=True))
    disk_speed = looked_up[0] / (looked_up[1] + 1.0 - active)
    push[...] = -CT_HALF * (disk_speed * jnp.abs(disk_speed)) * weight
    forced[...] = jnp.zeros_like(forced)

    def spread(group, carry):
        total = forced[...]
        for i in range(2):
            b = group * 2 + i
            high, low = split_points(pts[pl.ds(b, 1), :])
            hot = (iota((table_rows, SAMPLES), 0) == high).astype(jnp.float32).astype(jnp.bfloat16)
            value = push[pl.ds(b, 1), :]
            upper = value.astype(jnp.bfloat16).astype(jnp.float32)
            here = iota((LANES, SAMPLES), 0) == low
            placed = jnp.concatenate(
                [jnp.where(here, upper, 0.0), jnp.where(here, value - upper, 0.0)], axis=0
            ).astype(jnp.bfloat16)
            total = total + lax.dot_general(
                hot, placed, (((1,), (1,)), ((), ())), preferred_element_type=jnp.float32
            )
        forced[...] = total
        return carry

    lax.fori_loop(0, BLOCKS // 2, spread, 0)
    for i in range(ROTOR_TILES):
        lines = slice(i * ROTOR_LINES, (i + 1) * ROTOR_LINES)
        columns = slice(i * LANES, (i + 1) * LANES)
        advect[0:ROTOR_LINES, columns] += forced[lines, :LANES] + forced[lines, LANES:]

    for chunk in range(CHUNKS):
        arrived = back.at[:, chunk] if chunk < CHUNKS - 1 else last_back
        pltpu.make_async_copy(arrived, arrived, back_recv.at[chunk]).wait()
        if chunk < CHUNKS - 1:
            for half in range(2):
                combine(held, arrived.at[half], advect, result, chunk, half)

    for chunk in range(CHUNKS):
        others = pl.ds(0, PENCIL - PIECE)
        pltpu.make_async_copy(
            there.at[chunk, others], there.at[chunk, others], there_send.at[chunk]
        ).wait()
        pltpu.make_async_copy(
            sent.at[chunk, others], sent.at[chunk, others], back_send.at[chunk]
        ).wait()


def combine(held, arrived, advect, result, chunk, half):
    columns = pl.ds(half * HALF + chunk * CHUNK, CHUNK)
    across = held[PLANE : 2 * PLANE, columns].astype(jnp.float32)
    for f in range(FIELDS):
        lines = pl.ds(f * PLANE, PLANE)
        term = across * arrived[lines, :].astype(jnp.float32)
        result[lines, columns] = (advect[lines, columns] - term).astype(jnp.bfloat16)


def finish(held, last_back, advect, result, push, out, thrust_out, merged, out_sem):
    stores = [pltpu.make_async_copy(push, thrust_out, out_sem.at[0])]
    for half in range(2):
        early = pl.ds(half * HALF, HALF - CHUNK)
        stores.append(
            pltpu.make_async_copy(result.at[:, early], out.at[:, early], out_sem.at[1 + half])
        )
    for store in stores:
        store.start()
    for half in range(2):
        combine(held, last_back.at[half], advect, merged, CHUNKS - 1, half)
        late = pl.ds((half + 1) * HALF - CHUNK, CHUNK)
        stores.append(
            pltpu.make_async_copy(merged.at[:, late], out.at[:, late], out_sem.at[3 + half])
        )
        stores[-1].start()
    for store in stores:
        store.wait()


def per_device(fields, block_points, sample_weight, block_turbine, block_count):
    bf16, f32, i32 = jnp.bfloat16, jnp.float32, jnp.int32
    dma = pltpu.SemaphoreType.DMA
    parts = pl.pallas_call(
        kernel,
        out_shape=(
            pltpu.VMEM((ROWS, NX), bf16),
            pltpu.VMEM((2, ROWS, CHUNK), bf16),
            pltpu.VMEM((ROWS, NX), f32),
            pltpu.VMEM((ROWS, NX), bf16),
            pltpu.VMEM((BLOCKS, SAMPLES), f32),
        ),
        in_specs=[HBM] * 7,
        out_specs=(VMEM,) * 5,
        scratch_shapes=[
            pltpu.VMEM((CHUNKS, PENCIL, CHUNK), bf16),
            pltpu.VMEM((CHUNKS, PENCIL, CHUNK), bf16),
            pltpu.VMEM((2, CHUNKS - 1, ROWS, CHUNK), bf16),
            pltpu.VMEM((LANES, 2 * NX), f32),
            pltpu.VMEM((BAND, 2 * PENCIL - BAND), f32),
            pltpu.VMEM((LANES, 2 * NX), bf16),
            pltpu.VMEM((BAND, 2 * PENCIL - BAND), bf16),
            pltpu.VMEM((BLOCKS, SAMPLES), i32),
            pltpu.VMEM((BLOCKS, SAMPLES), bf16),
            pltpu.VMEM((N_COL, BLOCKS), i32),
            pltpu.VMEM((1, N_COL), i32),
            pltpu.VMEM((BLOCKS, SAMPLES), f32),
            pltpu.VMEM((LANES, ROTOR_TILES * ROTOR_LINES), bf16),
            pltpu.VMEM((ROTOR_TILES * ROTOR_LINES, 2 * LANES), f32),
            pltpu.VMEM((3, 8, LANES), f32),
            pltpu.VMEM((N_ROW - 1, 8, LANES), f32),
            pltpu.VMEM((RING_Y - 1, 8, LANES), f32),
            pltpu.VMEM((RING_Z - 1, 8, LANES), f32),
            dma((7,)),
            pltpu.SemaphoreType.REGULAR((3,)),
            dma((CHUNKS,)),
            dma((CHUNKS,)),
            dma((CHUNKS,)),
            dma((CHUNKS,)),
            dma((3,)),
            dma((3,)),
        ],
        compiler_params=pltpu.CompilerParams(
            collective_id=0, has_side_effects=True, vmem_limit_bytes=50 * 2**20
        ),
        name="advection",
    )(
        fields.reshape(ROWS, NX),
        block_points.reshape(BLOCKS, SAMPLES),
        sample_weight.reshape(BLOCKS, SAMPLES),
        block_turbine.reshape(N_COL, BLOCKS),
        block_count,
        jnp.asarray(band_x()),
        jnp.asarray(band_y()),
    )
    tendency, thrust = pl.pallas_call(
        finish,
        out_shape=(
            jax.ShapeDtypeStruct((ROWS, NX), bf16),
            jax.ShapeDtypeStruct((BLOCKS, SAMPLES), f32),
        ),
        in_specs=[VMEM] * 5,
        out_specs=(HBM, HBM),
        scratch_shapes=[pltpu.VMEM((ROWS, NX), bf16), dma((5,))],
        compiler_params=pltpu.CompilerParams(vmem_limit_bytes=16 * 2**20),
        name="finish",
    )(*parts)
    return tendency.reshape(fields.shape), thrust.reshape(block_points.shape)


def solution(mesh):
    placed = (
        P(None, "row", "col", None),
        P("row", "col", None, None),
        P("row", "col", None, None),
        P("row", None, None),
        P("row", None),
    )
    return jax.shard_map(
        per_device,
        mesh=mesh,
        in_specs=placed,
        out_specs=(P(None, "row", "col", None), P("row", "col", None, None)),
        check_vma=False,
    )
```

```python
import functools

import jax
import jax.numpy as jnp
import ml_dtypes
import numpy as np
from jax import lax
from jax.experimental import pallas as pl
from jax.experimental.pallas import tpu as pltpu
from jax.sharding import PartitionSpec as P

MESH = pl.DeviceIdType.MESH
HBM = pl.BlockSpec(memory_space=pltpu.HBM)
VMEM = pl.BlockSpec(memory_space=pltpu.VMEM)

N_ROW = 8
N_COL = 32
RING_Y = 4
RING_Z = 8
FIELDS = 4
NX = 1536
NY = 768
TURBINES = 400
BLOCKS = 48
SAMPLES = 256
LANES = 128
CT_HALF = 2.0 / 3.0
BUOYANCY = 0.3

ROWS = 768
PLANE = ROWS // FIELDS
PIECE = 2 * ROWS // N_COL
HALF = NX // 2
CHUNK = 256
CHUNKS = HALF // CHUNK
PENCIL = N_COL * PIECE
ROTOR_LINES = 16
ROTOR_TILES = NX // LANES
TURBINE_LANES = 512
BAND = 8 * PIECE
HUB_Z = 1


def spectral_row(length):
    offset = np.arange(length, dtype=np.int32)
    phase_angle = offset.astype(np.float32) * np.float32(np.pi / length)
    parity = np.float32(1.0) - np.float32(2.0) * (offset % 2).astype(np.float32)
    sine_safe = np.where(offset == 0, np.float32(1.0), np.sin(phase_angle))
    entries = np.float32(-(np.pi / length)) * parity * np.cos(phase_angle) / sine_safe
    entries = np.where(offset == 0, np.float32(0.0), entries)
    return entries.astype(ml_dtypes.bfloat16).astype(np.float32)


def band_x():
    m, i = np.arange(LANES)[:, None], np.arange(2 * NX)[None, :]
    return spectral_row(NX)[(m - i) % NX]


def band_y():
    depth = NY // N_COL
    r, s = np.arange(BAND)[:, None], np.arange(2 * PENCIL - BAND)[None, :] % PENCIL
    offset = (s // PIECE - r // PIECE) * depth + s % depth - r % depth
    same_level = (s % PIECE) // depth == (r % PIECE) // depth
    return np.where(same_level, spectral_row(NY)[offset % NY], np.float32(0.0))


def alternating(i):
    return lax.rem(jnp.where(i % 2 == 1, (i + 1) // 2, RING_Z - i // 2), RING_Z)


def iota(shape, dim):
    return lax.broadcasted_iota(jnp.int32, shape, dim)


def split_points(points):
    line = ((points >> 9) * 43) >> 7
    tile = (points >> 7) - line * ROTOR_TILES
    return tile * ROTOR_LINES + line, points & (LANES - 1)


def kernel(
    fields, points, weights, turbines, counts, wide_x, wide_y,
    held, last_back, advect, result, push,
    there, sent, back, stage_x, stage_y, tab_x, tab_y,
    pts, wts, trb, cnt, sampled, picked, forced, own, from_row, from_y, from_z, final,
    local_sem, known, there_send, there_recv, back_send, back_recv, sum_send, sum_recv,
):
    row = lax.axis_index("row")
    me = lax.axis_index("col")
    my_piece, my_half = me // 2, me % 2

    loads = [
        pltpu.make_async_copy(src, dst, local_sem.at[i])
        for i, (src, dst) in enumerate(
            [(fields, held), (points, pts), (weights, wts), (turbines, trb), (counts, cnt),
             (wide_x, stage_x), (wide_y, stage_y)]
        )
    ]

    z, y = me // RING_Y, me % RING_Y

    hub = z == HUB_Z

    def col_at(step_z, step_y):
        return lax.rem(z + step_z, RING_Z) * RING_Y + lax.rem(y + step_y, RING_Y)

    def greet(semaphore, steps):
        for step in steps:
            pl.semaphore_signal(
                semaphore, inc=1, device_id={"col": col_at(*step)}, device_id_type=MESH
            )

    def greet_row(k, carry):
        peer = lax.rem(row + k, N_ROW)
        pl.semaphore_signal(barrier, inc=1, device_id={"row": peer}, device_id_type=MESH)
        return carry

    def field_piece(peer, chunk):
        start = pl.multiple_of((peer % 2) * HALF + chunk * CHUNK, CHUNK)
        return fields.at[pl.ds((peer // 2) * PIECE, PIECE), pl.ds(start, CHUNK)]

    def send_there(peer, chunk):
        pltpu.make_async_remote_copy(
            src_ref=field_piece(peer, chunk),
            dst_ref=there.at[chunk, pl.ds(me * PIECE, PIECE)],
            send_sem=there_send.at[chunk],
            recv_sem=there_recv.at[chunk],
            device_id={"col": peer},
            device_id_type=MESH,
        ).start()

    barrier = pltpu.get_barrier_semaphore()
    beside = ((1, 0), (7, 0), (0, 1), (0, 3))
    greet(barrier, beside)

    @pl.when(hub)
    def _():
        lax.fori_loop(1, N_ROW, greet_row, 0)

    for load in loads:
        load.start()
    pl.semaphore_wait(barrier, len(beside) + jnp.where(hub, N_ROW - 1, 0))
    greet(known.at[0], beside)
    for step in beside:
        for chunk in range(CHUNKS):
            send_there(col_at(*step), chunk)
    pl.semaphore_wait(known.at[0], len(beside))
    two_away = ((2, 0), (6, 0), (0, 2))
    greet(known.at[1], two_away)
    for step in two_away + ((1, 1), (1, 3), (7, 1), (7, 3)):
        for chunk in range(CHUNKS):
            send_there(col_at(*step), chunk)
    pl.semaphore_wait(known.at[1], len(two_away))
    greet(known.at[2], two_away[:2])
    pl.semaphore_wait(known.at[2], 2)
    def send_rest(chunk):
        def send_far(i, carry):
            far = i // RING_Y
            send_there(col_at(jnp.where(far == 0, 4, 1 + 2 * far), i % RING_Y), chunk)
            return carry

        def send_middle(i, carry):
            send_there(col_at(2 + 4 * (i // 3), 1 + i % 3), chunk)
            return carry

        lax.fori_loop(0, 3 * RING_Y, send_far, 0)
        lax.fori_loop(0, 6, send_middle, 0)
        for step in ((1, 2), (7, 2)):
            send_there(col_at(*step), chunk)
        pltpu.make_async_copy(
            field_piece(me, chunk), there.at[chunk, pl.ds(me * PIECE, PIECE)], there_recv.at[chunk]
        ).start()

    send_rest(0)

    for load in loads[:5]:
        load.wait()
    lines = held[0:ROTOR_LINES, :].astype(jnp.float32)
    tiles = [lines[:, LANES * i : LANES * (i + 1)] for i in range(ROTOR_TILES)]
    picked[...] = jnp.concatenate(tiles, axis=0).T.astype(jnp.bfloat16)
    table_rows = ROTOR_TILES * ROTOR_LINES

    def pick(group, carry):
        for i in range(4):
            b = group * 4 + i
            high, low = split_points(pts[pl.ds(b, 1), :])
            hot = (iota((table_rows, SAMPLES), 0) == high).astype(jnp.float32).astype(jnp.bfloat16)
            columns = jnp.dot(picked[...], hot, preferred_element_type=jnp.float32)
            chosen = jnp.where(iota((LANES, SAMPLES), 0) == low, columns, 0.0)
            sampled[pl.ds(b, 1), :] = jnp.sum(chosen, axis=0, keepdims=True)
        return carry

    lax.fori_loop(0, BLOCKS // 4, pick, 0)

    count_here = jnp.sum(
        jnp.where(iota((1, N_COL), 1) == me, cnt[...], 0), axis=1, keepdims=True
    )
    active = (iota((BLOCKS, 1), 0) < count_here).astype(jnp.float32)
    weight = wts[...].astype(jnp.float32) * active
    turbine_row = trb[pl.ds(me, 1), :]
    diagonal = iota((BLOCKS, BLOCKS), 0) == iota((BLOCKS, BLOCKS), 1)
    turbine = jnp.sum(jnp.where(diagonal, turbine_row, 0), axis=1, keepdims=True)
    belongs = (iota((BLOCKS, TURBINE_LANES), 1) == turbine).astype(jnp.float32)
    moments = (
        jnp.sum(weight * sampled[...], axis=1, keepdims=True),
        jnp.sum(weight, axis=1, keepdims=True),
    )
    per_moment = TURBINE_LANES // LANES
    for m in range(2):
        partial = jnp.sum(belongs * moments[m], axis=0, keepdims=True)
        for i in range(per_moment):
            at = m * per_moment + i
            own[0, at : at + 1, :] = partial[:, LANES * i : LANES * (i + 1)]

    def tell(phase, source, slot, device):
        pltpu.make_async_remote_copy(
            src_ref=source,
            dst_ref=slot,
            send_sem=sum_send.at[phase],
            recv_sem=sum_recv.at[phase],
            device_id=device,
            device_id_type=MESH,
        ).start()

    def heard(phase, slots):
        pltpu.make_async_copy(slots, slots, sum_recv.at[phase]).wait()

    def told(phase, slots):
        pltpu.make_async_copy(slots, slots, sum_send.at[phase]).wait()

    for k in range(1, RING_Y):
        tell(0, own.at[0], from_y.at[k - 1], {"col": col_at(0, k)})
    send_rest(1)

    loads[5].wait()
    tab_x[...] = stage_x[...].astype(jnp.bfloat16)

    def along_x(i, carry):
        columns = pl.ds(pl.multiple_of(i * CHUNK, CHUNK), CHUNK)
        slices = [
            tab_x[:, pl.ds(pl.multiple_of(i * CHUNK + NX - LANES * a, LANES), CHUNK)]
            for a in range(NX // LANES)
        ]
        table = jnp.concatenate(slices, axis=0)
        speed = held[0:PLANE, columns].astype(jnp.float32)
        for f in range(FIELDS):
            lines = pl.ds(f * PLANE, PLANE)
            slope = jnp.dot(held[lines, :], table, preferred_element_type=jnp.float32)
            terms = -(speed * slope)
            if f == 2:
                heat = held[3 * PLANE : 4 * PLANE, columns].astype(jnp.float32)
                terms = terms + BUOYANCY * heat
            advect[lines, columns] = terms
        return carry

    lax.fori_loop(0, NX // CHUNK, along_x, 0)

    heard(0, from_y)
    own[1] = own[0] + jnp.sum(from_y[...], axis=0)

    @pl.when(z != HUB_Z)
    def _():
        slot = z - (z > HUB_Z).astype(jnp.int32)
        tell(1, own.at[1], from_z.at[slot], {"col": HUB_Z * RING_Y + y})

    send_rest(2)
    loads[6].wait()
    for i in range(8):
        lines = slice(i * PIECE, (i + 1) * PIECE)
        tab_y[lines, :] = stage_y[lines, :].astype(jnp.bfloat16)

    def along_y(chunk):
        pltpu.make_async_copy(there.at[chunk], there.at[chunk], there_recv.at[chunk]).wait()

        def tile(i, carry):
            start = pl.multiple_of(i * BAND, BAND)
            table = tab_y[:, pl.ds(pl.multiple_of((PENCIL - start) % PENCIL, BAND), PENCIL)]
            slope = jnp.dot(table, there[chunk], preferred_element_type=jnp.float32)
            sent[chunk, pl.ds(start, BAND), :] = slope.astype(jnp.bfloat16)
            return carry

        lax.fori_loop(0, PENCIL // BAND, tile, 0)
        lines = pl.ds(my_piece * PIECE, PIECE)
        if chunk < CHUNKS - 1:
            landing = back.at[my_half, chunk, lines]
        else:
            landing = last_back.at[my_half, lines]

        def send_back(k, carry):
            peer = k - 1 + (k - 1 >= me).astype(jnp.int32)
            pltpu.make_async_remote_copy(
                src_ref=sent.at[chunk, pl.ds(peer * PIECE, PIECE)],
                dst_ref=landing,
                send_sem=back_send.at[chunk],
                recv_sem=back_recv.at[chunk],
                device_id={"col": peer},
                device_id_type=MESH,
            ).start()
            return carry

        lax.fori_loop(1, N_COL, send_back, 0)
        pltpu.make_async_copy(
            sent.at[chunk, pl.ds(me * PIECE, PIECE)], landing, back_recv.at[chunk]
        ).start()

    @pl.when(hub)
    def _():
        heard(1, from_z)
        own[2] = own[1] + jnp.sum(from_z[...], axis=0)
        for k in range(1, N_ROW):
            tell(2, own.at[2], from_row.at[k - 1], {"row": lax.rem(row + k, N_ROW)})
        heard(2, from_row)
        final[...] = own[2] + jnp.sum(from_row[...], axis=0)
        for k in range(1, RING_Z):
            tell(3, final, final, {"col": col_at(k, 0)})

    for chunk in range(CHUNKS):
        along_y(chunk)

    @pl.when(z != HUB_Z)
    def _():
        heard(3, final)

    totals = final[...]
    looked_up = []
    for m in range(2):
        parts = [totals[m * per_moment + i : m * per_moment + i + 1, :] for i in range(per_moment)]
        found = belongs * jnp.concatenate(parts, axis=1)
        looked_up.append(jnp.sum(found, axis=1, keepdims=True))
    disk_speed = looked_up[0] / (looked_up[1] + 1.0 - active)
    push[...] = -CT_HALF * (disk_speed * jnp.abs(disk_speed)) * weight
    forced[...] = jnp.zeros_like(forced)

    def spread(group, carry):
        total = forced[...]
        for i in range(2):
            b = group * 2 + i
            high, low = split_points(pts[pl.ds(b, 1), :])
            hot = (iota((table_rows, SAMPLES), 0) == high).astype(jnp.float32).astype(jnp.bfloat16)
            value = push[pl.ds(b, 1), :]
            upper = value.astype(jnp.bfloat16).astype(jnp.float32)
            here = iota((LANES, SAMPLES), 0) == low
            placed = jnp.concatenate(
                [jnp.where(here, upper, 0.0), jnp.where(here, value - upper, 0.0)], axis=0
            ).astype(jnp.bfloat16)
            total = total + lax.dot_general(
                hot, placed, (((1,), (1,)), ((), ())), preferred_element_type=jnp.float32
            )
        forced[...] = total
        return carry

    lax.fori_loop(0, BLOCKS // 2, spread, 0)
    for i in range(ROTOR_TILES):
        lines = slice(i * ROTOR_LINES, (i + 1) * ROTOR_LINES)
        columns = slice(i * LANES, (i + 1) * LANES)
        advect[0:ROTOR_LINES, columns] += forced[lines, :LANES] + forced[lines, LANES:]

    told(0, from_y)

    @pl.when(z != HUB_Z)
    def _():
        told(1, from_z.at[0])

    @pl.when(hub)
    def _():
        told(2, from_row)
        told(3, from_z)

    for chunk in range(CHUNKS):
        arrived = back.at[:, chunk] if chunk < CHUNKS - 1 else last_back
        pltpu.make_async_copy(arrived, arrived, back_recv.at[chunk]).wait()
        if chunk < CHUNKS - 1:
            for half in range(2):
                combine(held, arrived.at[half], advect, result, chunk, half)

    for chunk in range(CHUNKS):
        others = pl.ds(0, PENCIL - PIECE)
        pltpu.make_async_copy(
            there.at[chunk, others], there.at[chunk, others], there_send.at[chunk]
        ).wait()
        pltpu.make_async_copy(
            sent.at[chunk, others], sent.at[chunk, others], back_send.at[chunk]
        ).wait()


def combine(held, arrived, advect, result, chunk, half):
    columns = pl.ds(half * HALF + chunk * CHUNK, CHUNK)
    across = held[PLANE : 2 * PLANE, columns].astype(jnp.float32)
    for f in range(FIELDS):
        lines = pl.ds(f * PLANE, PLANE)
        term = across * arrived[lines, :].astype(jnp.float32)
        result[lines, columns] = (advect[lines, columns] - term).astype(jnp.bfloat16)


def finish(held, last_back, advect, result, push, out, thrust_out, merged, out_sem):
    stores = [pltpu.make_async_copy(push, thrust_out, out_sem.at[0])]
    for half in range(2):
        early = pl.ds(half * HALF, HALF - CHUNK)
        stores.append(
            pltpu.make_async_copy(result.at[:, early], out.at[:, early], out_sem.at[1 + half])
        )
    for store in stores:
        store.start()
    for half in range(2):
        combine(held, last_back.at[half], advect, merged, CHUNKS - 1, half)
        late = pl.ds((half + 1) * HALF - CHUNK, CHUNK)
        stores.append(
            pltpu.make_async_copy(merged.at[:, late], out.at[:, late], out_sem.at[3 + half])
        )
        stores[-1].start()
    for store in stores:
        store.wait()


def per_device(fields, block_points, sample_weight, block_turbine, block_count):
    bf16, f32, i32 = jnp.bfloat16, jnp.float32, jnp.int32
    dma = pltpu.SemaphoreType.DMA
    parts = pl.pallas_call(
        kernel,
        out_shape=(
            pltpu.VMEM((ROWS, NX), bf16),
            pltpu.VMEM((2, ROWS, CHUNK), bf16),
            pltpu.VMEM((ROWS, NX), f32),
            pltpu.VMEM((ROWS, NX), bf16),
            pltpu.VMEM((BLOCKS, SAMPLES), f32),
        ),
        in_specs=[HBM] * 7,
        out_specs=(VMEM,) * 5,
        scratch_shapes=[
            pltpu.VMEM((CHUNKS, PENCIL, CHUNK), bf16),
            pltpu.VMEM((CHUNKS, PENCIL, CHUNK), bf16),
            pltpu.VMEM((2, CHUNKS - 1, ROWS, CHUNK), bf16),
            pltpu.VMEM((LANES, 2 * NX), f32),
            pltpu.VMEM((BAND, 2 * PENCIL - BAND), f32),
            pltpu.VMEM((LANES, 2 * NX), bf16),
            pltpu.VMEM((BAND, 2 * PENCIL - BAND), bf16),
            pltpu.VMEM((BLOCKS, SAMPLES), i32),
            pltpu.VMEM((BLOCKS, SAMPLES), bf16),
            pltpu.VMEM((N_COL, BLOCKS), i32),
            pltpu.VMEM((1, N_COL), i32),
            pltpu.VMEM((BLOCKS, SAMPLES), f32),
            pltpu.VMEM((LANES, ROTOR_TILES * ROTOR_LINES), bf16),
            pltpu.VMEM((ROTOR_TILES * ROTOR_LINES, 2 * LANES), f32),
            pltpu.VMEM((3, 8, LANES), f32),
            pltpu.VMEM((N_ROW - 1, 8, LANES), f32),
            pltpu.VMEM((RING_Y - 1, 8, LANES), f32),
            pltpu.VMEM((RING_Z - 1, 8, LANES), f32),
            pltpu.VMEM((8, LANES), f32),
            dma((7,)),
            pltpu.SemaphoreType.REGULAR((3,)),
            dma((CHUNKS,)),
            dma((CHUNKS,)),
            dma((CHUNKS,)),
            dma((CHUNKS,)),
            dma((4,)),
            dma((4,)),
        ],
        compiler_params=pltpu.CompilerParams(
            collective_id=0, has_side_effects=True, vmem_limit_bytes=50 * 2**20
        ),
        name="advection",
    )(
        fields.reshape(ROWS, NX),
        block_points.reshape(BLOCKS, SAMPLES),
        sample_weight.reshape(BLOCKS, SAMPLES),
        block_turbine.reshape(N_COL, BLOCKS),
        block_count,
        jnp.asarray(band_x()),
        jnp.asarray(band_y()),
    )
    tendency, thrust = pl.pallas_call(
        finish,
        out_shape=(
            jax.ShapeDtypeStruct((ROWS, NX), bf16),
            jax.ShapeDtypeStruct((BLOCKS, SAMPLES), f32),
        ),
        in_specs=[VMEM] * 5,
        out_specs=(HBM, HBM),
        scratch_shapes=[pltpu.VMEM((ROWS, NX), bf16), dma((5,))],
        compiler_params=pltpu.CompilerParams(vmem_limit_bytes=16 * 2**20),
        name="finish",
    )(*parts)
    return tendency.reshape(fields.shape), thrust.reshape(block_points.shape)


def solution(mesh):
    placed = (
        P(None, "row", "col", None),
        P("row", "col", None, None),
        P("row", "col", None, None),
        P("row", None, None),
        P("row", None),
    )
    return jax.shard_map(
        per_device,
        mesh=mesh,
        in_specs=placed,
        out_specs=(P(None, "row", "col", None), P("row", "col", None, None)),
        check_vma=False,
    )
```

```python
import functools

import jax
import jax.numpy as jnp
import ml_dtypes
import numpy as np
from jax import lax
from jax.experimental import pallas as pl
from jax.experimental.pallas import tpu as pltpu
from jax.sharding import PartitionSpec as P

MESH = pl.DeviceIdType.MESH
HBM = pl.BlockSpec(memory_space=pltpu.HBM)
VMEM = pl.BlockSpec(memory_space=pltpu.VMEM)

N_ROW = 8
N_COL = 32
RING_Y = 4
RING_Z = 8
FIELDS = 4
NX = 1536
NY = 768
TURBINES = 400
BLOCKS = 48
SAMPLES = 256
LANES = 128
CT_HALF = 2.0 / 3.0
BUOYANCY = 0.3

ROWS = 768
PLANE = ROWS // FIELDS
PIECE = 2 * ROWS // N_COL
HALF = NX // 2
CHUNK = 256
CHUNKS = HALF // CHUNK
PENCIL = N_COL * PIECE
ROTOR_LINES = 16
ROTOR_TILES = NX // LANES
TURBINE_LANES = 512
BAND = 8 * PIECE
HUB_Z = 1


def spectral_row(length):
    offset = np.arange(length, dtype=np.int32)
    phase_angle = offset.astype(np.float32) * np.float32(np.pi / length)
    parity = np.float32(1.0) - np.float32(2.0) * (offset % 2).astype(np.float32)
    sine_safe = np.where(offset == 0, np.float32(1.0), np.sin(phase_angle))
    entries = np.float32(-(np.pi / length)) * parity * np.cos(phase_angle) / sine_safe
    entries = np.where(offset == 0, np.float32(0.0), entries)
    return entries.astype(ml_dtypes.bfloat16).astype(np.float32)


def band_x():
    m, i = np.arange(LANES)[:, None], np.arange(2 * NX)[None, :]
    return spectral_row(NX)[(m - i) % NX]


def band_y():
    depth = NY // N_COL
    r, s = np.arange(BAND)[:, None], np.arange(2 * PENCIL - BAND)[None, :] % PENCIL
    offset = (s // PIECE - r // PIECE) * depth + s % depth - r % depth
    same_level = (s % PIECE) // depth == (r % PIECE) // depth
    return np.where(same_level, spectral_row(NY)[offset % NY], np.float32(0.0))


def alternating(i):
    return lax.rem(jnp.where(i % 2 == 1, (i + 1) // 2, RING_Z - i // 2), RING_Z)


def iota(shape, dim):
    return lax.broadcasted_iota(jnp.int32, shape, dim)


def split_points(points):
    line = ((points >> 9) * 43) >> 7
    tile = (points >> 7) - line * ROTOR_TILES
    return tile * ROTOR_LINES + line, points & (LANES - 1)


def kernel(
    fields, points, weights, turbines, counts, wide_x, wide_y,
    held, last_back, advect, result, push,
    there, sent, back, stage_x, stage_y, tab_x, tab_y,
    pts, wts, trb, cnt, sampled, picked, forced, own, from_row, from_y, from_z, final,
    local_sem, known, there_send, there_recv, back_send, back_recv, sum_send, sum_recv,
):
    row = lax.axis_index("row")
    me = lax.axis_index("col")
    my_piece, my_half = me // 2, me % 2

    loads = [
        pltpu.make_async_copy(src, dst, local_sem.at[i])
        for i, (src, dst) in enumerate(
            [(fields, held), (points, pts), (weights, wts), (turbines, trb), (counts, cnt),
             (wide_x, stage_x), (wide_y, stage_y)]
        )
    ]

    z, y = me // RING_Y, me % RING_Y

    hub = z == HUB_Z

    def col_at(step_z, step_y):
        return lax.rem(z + step_z, RING_Z) * RING_Y + lax.rem(y + step_y, RING_Y)

    def greet(semaphore, steps):
        for step in steps:
            pl.semaphore_signal(
                semaphore, inc=1, device_id={"col": col_at(*step)}, device_id_type=MESH
            )

    def greet_row(k, carry):
        peer = lax.rem(row + k, N_ROW)
        pl.semaphore_signal(barrier, inc=1, device_id={"row": peer}, device_id_type=MESH)
        return carry

    def field_piece(peer, chunk):
        start = pl.multiple_of((peer % 2) * HALF + chunk * CHUNK, CHUNK)
        return fields.at[pl.ds((peer // 2) * PIECE, PIECE), pl.ds(start, CHUNK)]

    def send_there(peer, chunk):
        pltpu.make_async_remote_copy(
            src_ref=field_piece(peer, chunk),
            dst_ref=there.at[chunk, pl.ds(me * PIECE, PIECE)],
            send_sem=there_send.at[chunk],
            recv_sem=there_recv.at[chunk],
            device_id={"col": peer},
            device_id_type=MESH,
        ).start()

    barrier = pltpu.get_barrier_semaphore()
    beside = ((1, 0), (7, 0), (0, 1), (0, 3))
    greet(barrier, beside)

    @pl.when(hub)
    def _():
        lax.fori_loop(1, N_ROW, greet_row, 0)

    for load in loads:
        load.start()
    pl.semaphore_wait(barrier, len(beside) + jnp.where(hub, N_ROW - 1, 0))
    greet(known.at[0], beside)
    for step in beside:
        for chunk in range(CHUNKS):
            send_there(col_at(*step), chunk)
    pl.semaphore_wait(known.at[0], len(beside))
    two_away = ((2, 0), (6, 0), (0, 2))
    greet(known.at[1], two_away)
    for step in two_away + ((1, 1), (1, 3), (7, 1), (7, 3)):
        for chunk in range(CHUNKS):
            send_there(col_at(*step), chunk)
    pl.semaphore_wait(known.at[1], len(two_away))
    greet(known.at[2], two_away[:2])
    pl.semaphore_wait(known.at[2], 2)
    def send_rest(chunk):
        def send_far(i, carry):
            far = i // RING_Y
            send_there(col_at(jnp.where(far == 0, 4, 1 + 2 * far), i % RING_Y), chunk)
            return carry

        def send_middle(i, carry):
            send_there(col_at(2 + 4 * (i // 3), 1 + i % 3), chunk)
            return carry

        lax.fori_loop(0, 3 * RING_Y, send_far, 0)
        lax.fori_loop(0, 6, send_middle, 0)
        for step in ((1, 2), (7, 2)):
            send_there(col_at(*step), chunk)
        pltpu.make_async_copy(
            field_piece(me, chunk), there.at[chunk, pl.ds(me * PIECE, PIECE)], there_recv.at[chunk]
        ).start()

    send_rest(0)

    for load in loads[:5]:
        load.wait()
    lines = held[0:ROTOR_LINES, :].astype(jnp.float32)
    tiles = [lines[:, LANES * i : LANES * (i + 1)] for i in range(ROTOR_TILES)]
    picked[...] = jnp.concatenate(tiles, axis=0).T.astype(jnp.bfloat16)
    table_rows = ROTOR_TILES * ROTOR_LINES

    def pick(group, carry):
        for i in range(4):
            b = group * 4 + i
            high, low = split_points(pts[pl.ds(b, 1), :])
            hot = (iota((table_rows, SAMPLES), 0) == high).astype(jnp.float32).astype(jnp.bfloat16)
            columns = jnp.dot(picked[...], hot, preferred_element_type=jnp.float32)
            chosen = jnp.where(iota((LANES, SAMPLES), 0) == low, columns, 0.0)
            sampled[pl.ds(b, 1), :] = jnp.sum(chosen, axis=0, keepdims=True)
        return carry

    lax.fori_loop(0, BLOCKS // 4, pick, 0)

    count_here = jnp.sum(
        jnp.where(iota((1, N_COL), 1) == me, cnt[...], 0), axis=1, keepdims=True
    )
    active = (iota((BLOCKS, 1), 0) < count_here).astype(jnp.float32)
    weight = wts[...].astype(jnp.float32) * active
    turbine_row = trb[pl.ds(me, 1), :]
    diagonal = iota((BLOCKS, BLOCKS), 0) == iota((BLOCKS, BLOCKS), 1)
    turbine = jnp.sum(jnp.where(diagonal, turbine_row, 0), axis=1, keepdims=True)
    belongs = (iota((BLOCKS, TURBINE_LANES), 1) == turbine).astype(jnp.float32)
    moments = (
        jnp.sum(weight * sampled[...], axis=1, keepdims=True),
        jnp.sum(weight, axis=1, keepdims=True),
    )
    per_moment = TURBINE_LANES // LANES
    for m in range(2):
        partial = jnp.sum(belongs * moments[m], axis=0, keepdims=True)
        for i in range(per_moment):
            at = m * per_moment + i
            own[0, at : at + 1, :] = partial[:, LANES * i : LANES * (i + 1)]

    def tell(phase, source, slot, device):
        pltpu.make_async_remote_copy(
            src_ref=source,
            dst_ref=slot,
            send_sem=sum_send.at[phase],
            recv_sem=sum_recv.at[phase],
            device_id=device,
            device_id_type=MESH,
        ).start()

    def heard(phase, slots):
        pltpu.make_async_copy(slots, slots, sum_recv.at[phase]).wait()

    def told(phase, slots):
        pltpu.make_async_copy(slots, slots, sum_send.at[phase]).wait()

    for k in range(1, RING_Y):
        tell(0, own.at[0], from_y.at[k - 1], {"col": col_at(0, k)})
    send_rest(1)

    loads[5].wait()
    tab_x[...] = stage_x[...].astype(jnp.bfloat16)

    def along_x(i, carry):
        columns = pl.ds(pl.multiple_of(i * CHUNK, CHUNK), CHUNK)
        slices = [
            tab_x[:, pl.ds(pl.multiple_of(i * CHUNK + NX - LANES * a, LANES), CHUNK)]
            for a in range(NX // LANES)
        ]
        table = jnp.concatenate(slices, axis=0)
        speed = held[0:PLANE, columns].astype(jnp.float32)
        for f in range(FIELDS):
            lines = pl.ds(f * PLANE, PLANE)
            slope = jnp.dot(held[lines, :], table, preferred_element_type=jnp.float32)
            terms = -(speed * slope)
            if f == 2:
                heat = held[3 * PLANE : 4 * PLANE, columns].astype(jnp.float32)
                terms = terms + BUOYANCY * heat
            advect[lines, columns] = terms
        return carry

    lax.fori_loop(0, NX // CHUNK, along_x, 0)

    heard(0, from_y)
    own[1] = own[0] + jnp.sum(from_y[...], axis=0)

    @pl.when(z != HUB_Z)
    def _():
        slot = z - (z > HUB_Z).astype(jnp.int32)
        tell(1, own.at[1], from_z.at[slot], {"col": HUB_Z * RING_Y + y})

    send_rest(2)
    loads[6].wait()
    for i in range(8):
        lines = slice(i * PIECE, (i + 1) * PIECE)
        tab_y[lines, :] = stage_y[lines, :].astype(jnp.bfloat16)

    def along_y(chunk):
        pltpu.make_async_copy(there.at[chunk], there.at[chunk], there_recv.at[chunk]).wait()

        def tile(i, carry):
            start = pl.multiple_of(i * BAND, BAND)
            table = tab_y[:, pl.ds(pl.multiple_of((PENCIL - start) % PENCIL, BAND), PENCIL)]
            slope = jnp.dot(table, there[chunk], preferred_element_type=jnp.float32)
            sent[chunk, pl.ds(start, BAND), :] = slope.astype(jnp.bfloat16)
            return carry

        lax.fori_loop(0, PENCIL // BAND, tile, 0)
        lines = pl.ds(my_piece * PIECE, PIECE)
        if chunk < CHUNKS - 1:
            landing = back.at[my_half, chunk, lines]
        else:
            landing = last_back.at[my_half, lines]

        def send_back(k, carry):
            shifted = row % 2 == 1
            rank = jnp.where(z == 2, 0, jnp.where(z < 2, z + 1, z))
            own_place = jnp.where(shifted, rank, z) * RING_Y + y
            place = k - 1 + (k - 1 >= own_place).astype(jnp.int32)
            group = place // RING_Y
            moved = jnp.where(group == 0, 2, jnp.where(group <= 2, group - 1, group))
            peer = jnp.where(shifted, moved, group) * RING_Y + place % RING_Y
            pltpu.make_async_remote_copy(
                src_ref=sent.at[chunk, pl.ds(peer * PIECE, PIECE)],
                dst_ref=landing,
                send_sem=back_send.at[chunk],
                recv_sem=back_recv.at[chunk],
                device_id={"col": peer},
                device_id_type=MESH,
            ).start()
            return carry

        lax.fori_loop(1, N_COL, send_back, 0)
        pltpu.make_async_copy(
            sent.at[chunk, pl.ds(me * PIECE, PIECE)], landing, back_recv.at[chunk]
        ).start()

    @pl.when(hub)
    def _():
        heard(1, from_z)
        own[2] = own[1] + jnp.sum(from_z[...], axis=0)
        for k in range(1, N_ROW):
            tell(2, own.at[2], from_row.at[k - 1], {"row": lax.rem(row + k, N_ROW)})
        heard(2, from_row)
        final[...] = own[2] + jnp.sum(from_row[...], axis=0)
        for k in range(1, RING_Z):
            tell(3, final, final, {"col": col_at(k, 0)})

    for chunk in range(CHUNKS):
        along_y(chunk)

    @pl.when(z != HUB_Z)
    def _():
        heard(3, final)

    totals = final[...]
    looked_up = []
    for m in range(2):
        parts = [totals[m * per_moment + i : m * per_moment + i + 1, :] for i in range(per_moment)]
        found = belongs * jnp.concatenate(parts, axis=1)
        looked_up.append(jnp.sum(found, axis=1, keepdims=True))
    disk_speed = looked_up[0] / (looked_up[1] + 1.0 - active)
    push[...] = -CT_HALF * (disk_speed * jnp.abs(disk_speed)) * weight
    forced[...] = jnp.zeros_like(forced)

    def spread(group, carry):
        total = forced[...]
        for i in range(2):
            b = group * 2 + i
            high, low = split_points(pts[pl.ds(b, 1), :])
            hot = (iota((table_rows, SAMPLES), 0) == high).astype(jnp.float32).astype(jnp.bfloat16)
            value = push[pl.ds(b, 1), :]
            upper = value.astype(jnp.bfloat16).astype(jnp.float32)
            here = iota((LANES, SAMPLES), 0) == low
            placed = jnp.concatenate(
                [jnp.where(here, upper, 0.0), jnp.where(here, value - upper, 0.0)], axis=0
            ).astype(jnp.bfloat16)
            total = total + lax.dot_general(
                hot, placed, (((1,), (1,)), ((), ())), preferred_element_type=jnp.float32
            )
        forced[...] = total
        return carry

    lax.fori_loop(0, BLOCKS // 2, spread, 0)
    for i in range(ROTOR_TILES):
        lines = slice(i * ROTOR_LINES, (i + 1) * ROTOR_LINES)
        columns = slice(i * LANES, (i + 1) * LANES)
        advect[0:ROTOR_LINES, columns] += forced[lines, :LANES] + forced[lines, LANES:]

    told(0, from_y)

    @pl.when(z != HUB_Z)
    def _():
        told(1, from_z.at[0])

    @pl.when(hub)
    def _():
        told(2, from_row)
        told(3, from_z)

    def wait_sends():
        for chunk in range(CHUNKS):
            others = pl.ds(0, PENCIL - PIECE)
            pltpu.make_async_copy(
                there.at[chunk, others], there.at[chunk, others], there_send.at[chunk]
            ).wait()
            pltpu.make_async_copy(
                sent.at[chunk, others], sent.at[chunk, others], back_send.at[chunk]
            ).wait()

    for chunk in range(CHUNKS):
        if chunk == CHUNKS - 1:
            wait_sends()
        arrived = back.at[:, chunk] if chunk < CHUNKS - 1 else last_back
        pltpu.make_async_copy(arrived, arrived, back_recv.at[chunk]).wait()
        if chunk < CHUNKS - 1:
            for half in range(2):
                combine(held, arrived.at[half], advect, result, chunk, half)


def combine(held, arrived, advect, result, chunk, half):
    columns = pl.ds(half * HALF + chunk * CHUNK, CHUNK)
    across = held[PLANE : 2 * PLANE, columns].astype(jnp.float32)
    for f in range(FIELDS):
        lines = pl.ds(f * PLANE, PLANE)
        term = across * arrived[lines, :].astype(jnp.float32)
        result[lines, columns] = (advect[lines, columns] - term).astype(jnp.bfloat16)


def finish(held, last_back, advect, result, push, out, thrust_out, merged, out_sem):
    stores = [pltpu.make_async_copy(push, thrust_out, out_sem.at[0])]
    for half in range(2):
        early = pl.ds(half * HALF, HALF - CHUNK)
        stores.append(
            pltpu.make_async_copy(result.at[:, early], out.at[:, early], out_sem.at[1 + half])
        )
    for store in stores:
        store.start()
    for half in range(2):
        combine(held, last_back.at[half], advect, merged, CHUNKS - 1, half)
        late = pl.ds((half + 1) * HALF - CHUNK, CHUNK)
        stores.append(
            pltpu.make_async_copy(merged.at[:, late], out.at[:, late], out_sem.at[3 + half])
        )
        stores[-1].start()
    for store in stores:
        store.wait()


def per_device(fields, block_points, sample_weight, block_turbine, block_count):
    bf16, f32, i32 = jnp.bfloat16, jnp.float32, jnp.int32
    dma = pltpu.SemaphoreType.DMA
    parts = pl.pallas_call(
        kernel,
        out_shape=(
            pltpu.VMEM((ROWS, NX), bf16),
            pltpu.VMEM((2, ROWS, CHUNK), bf16),
            pltpu.VMEM((ROWS, NX), f32),
            pltpu.VMEM((ROWS, NX), bf16),
            pltpu.VMEM((BLOCKS, SAMPLES), f32),
        ),
        in_specs=[HBM] * 7,
        out_specs=(VMEM,) * 5,
        scratch_shapes=[
            pltpu.VMEM((CHUNKS, PENCIL, CHUNK), bf16),
            pltpu.VMEM((CHUNKS, PENCIL, CHUNK), bf16),
            pltpu.VMEM((2, CHUNKS - 1, ROWS, CHUNK), bf16),
            pltpu.VMEM((LANES, 2 * NX), f32),
            pltpu.VMEM((BAND, 2 * PENCIL - BAND), f32),
            pltpu.VMEM((LANES, 2 * NX), bf16),
            pltpu.VMEM((BAND, 2 * PENCIL - BAND), bf16),
            pltpu.VMEM((BLOCKS, SAMPLES), i32),
            pltpu.VMEM((BLOCKS, SAMPLES), bf16),
            pltpu.VMEM((N_COL, BLOCKS), i32),
            pltpu.VMEM((1, N_COL), i32),
            pltpu.VMEM((BLOCKS, SAMPLES), f32),
            pltpu.VMEM((LANES, ROTOR_TILES * ROTOR_LINES), bf16),
            pltpu.VMEM((ROTOR_TILES * ROTOR_LINES, 2 * LANES), f32),
            pltpu.VMEM((3, 8, LANES), f32),
            pltpu.VMEM((N_ROW - 1, 8, LANES), f32),
            pltpu.VMEM((RING_Y - 1, 8, LANES), f32),
            pltpu.VMEM((RING_Z - 1, 8, LANES), f32),
            pltpu.VMEM((8, LANES), f32),
            dma((7,)),
            pltpu.SemaphoreType.REGULAR((3,)),
            dma((CHUNKS,)),
            dma((CHUNKS,)),
            dma((CHUNKS,)),
            dma((CHUNKS,)),
            dma((4,)),
            dma((4,)),
        ],
        compiler_params=pltpu.CompilerParams(
            collective_id=0, has_side_effects=True, vmem_limit_bytes=50 * 2**20
        ),
        name="advection",
    )(
        fields.reshape(ROWS, NX),
        block_points.reshape(BLOCKS, SAMPLES),
        sample_weight.reshape(BLOCKS, SAMPLES),
        block_turbine.reshape(N_COL, BLOCKS),
        block_count,
        jnp.asarray(band_x()),
        jnp.asarray(band_y()),
    )
    tendency, thrust = pl.pallas_call(
        finish,
        out_shape=(
            jax.ShapeDtypeStruct((ROWS, NX), bf16),
            jax.ShapeDtypeStruct((BLOCKS, SAMPLES), f32),
        ),
        in_specs=[VMEM] * 5,
        out_specs=(HBM, HBM),
        scratch_shapes=[pltpu.VMEM((ROWS, NX), bf16), dma((5,))],
        compiler_params=pltpu.CompilerParams(vmem_limit_bytes=16 * 2**20),
        name="finish",
    )(*parts)
    return tendency.reshape(fields.shape), thrust.reshape(block_points.shape)


def solution(mesh):
    placed = (
        P(None, "row", "col", None),
        P("row", "col", None, None),
        P("row", "col", None, None),
        P("row", None, None),
        P("row", None),
    )
    return jax.shard_map(
        per_device,
        mesh=mesh,
        in_specs=placed,
        out_specs=(P(None, "row", "col", None), P("row", "col", None, None)),
        check_vma=False,
    )
```
